32 devices in a mesh: grp: 2 (over x), gz: 16 (over z, y, core).
Axes of the slice: x: 2, y: 2, z: 4, core: 2. Of those that a mesh axis runs over, the one named last changes fastest.
Arguments:
- spectra: float32 [2048, 4096], P(('grp', 'gz')), parts along dimension 0, may hold values from -6 to 6
- offsets: int32 [2048], P(('grp', 'gz')), parts along dimension 0, may hold values from 0 to 8192, as said below
- mask_bits: int32 [2048, 256], P(('grp', 'gz')), parts along dimension 0, may hold values from 0 to 65535
- eigen: float32 [16, 12288], P(None, 'gz'), as said below
- plan: int32 [16, 3], P('grp'), parts along dimension 0, may hold values from 0 to 15, as said below
Outputs:
- coefficients: float32 [32, 5, 256], P(('grp', 'gz')), parts along dimension 0
- eigen_new: float32 [32, 12288], P('grp', 'gz'), parts along dimension 0
The draws below stay inside these ranges and needn't reach their ends.
There are 2 independent parts, one for each index of `grp`. The reference program is written for one: setup_inputs(seed, part) draws one part's arguments, and reference() takes and returns one part's arrays. A program takes and returns all parts, laid end to end along the dimension named above; an argument that names none is the same for every part. Nothing has to cross between parts.
Inputs may be any that keep to these rules, and one draw needn't show every extreme that they name: `offsets`: offset of spectrum g lies between g * 8064 // 1024 and that plus 128; the first spectrum's offset is 0 and the last one's 12288 - 4096. `plan`: row j names devices j and j + 8 (one as source, the other as destination, in either order) and then a block number below 4. `eigen`: rows of the eigenspectra have scales that vary over the pixels.
All inputs are finite; a program needn't handle non-finite values.
Results may differ from the reference program's by a relative error of at most 0.0003.
Values sent between devices are 32-bit elements; how exact they have to be, the bound alone decides.
A program may use at most 64 MiB of HBM per device.

```python
import math
import jax
import jax.numpy as jnp
from jax import lax

K = 16
P_SIZE = 12288
W = 4096
NB = 4
BS = 16
SPAN = 128
S_TOTAL = 1024
PAIRS = 8
N_GZ = 16


def draw_eigen(key, part):
    first, second, third = jax.random.split(key, 3)
    place = jnp.arange(P_SIZE, dtype=jnp.float32) / P_SIZE
    base = jax.random.normal(first, (K, P_SIZE), jnp.float32)
    rows = 0.4 * jnp.exp(2.3025851 * place)
    rough = jnp.exp(jax.random.uniform(second, (1, P_SIZE), jnp.float32, -0.4, 0.4))
    columns = jnp.exp(jax.random.uniform(third, (K, 1), jnp.float32, -0.7, 0.7))
    return base * rows[None, :] * rough * columns


def draw_offsets(key, part):
    order = jnp.arange(S_TOTAL, dtype=jnp.int32)
    ramp = order * (P_SIZE - W - SPAN) // S_TOTAL
    jitter = jax.random.randint(key, (S_TOTAL,), 0, SPAN + 1, dtype=jnp.int32)
    starts = ramp + jitter
    starts = starts.at[0].set(0)
    starts = starts.at[S_TOTAL - 1].set(P_SIZE - W)
    return starts


def draw_plan(key, part):
    first, second = jax.random.split(jax.random.fold_in(key, 7))
    rows = jnp.arange(PAIRS, dtype=jnp.int32)
    flips = jax.random.randint(first, (PAIRS,), 0, 2, dtype=jnp.int32)
    source = rows + flips * PAIRS
    target = rows + (1 - flips) * PAIRS
    blocks = jax.random.randint(second, (PAIRS,), 0, NB, dtype=jnp.int32)
    return jnp.stack([source, target, blocks], axis=1)


def with_ends(drawn, own_key, least, largest):
    index_at = [jax.random.randint(jax.random.fold_in(own_key, axis), (), 0, length) for axis, length in enumerate(drawn.shape)]
    main_axis = drawn.shape.index(max(drawn.shape))
    beside = index_at[:main_axis] + [(index_at[main_axis] + 1) % drawn.shape[main_axis]] + index_at[main_axis + 1:]
    return drawn.at[tuple(index_at)].set(least).at[tuple(beside)].set(largest)


def block_levels(stream_key, dims, cuts, smallest, largest):
    gain = 1.0
    for axis_at, parts in cuts:
        steps = jax.random.uniform(jax.random.fold_in(jax.random.fold_in(stream_key, 6), axis_at), (parts,), jnp.float32, smallest / len(cuts), largest / len(cuts))
        gain = gain * jnp.repeat(jnp.exp(steps), dims[axis_at] // parts).reshape((-1,) + (1,) * (len(dims) - 1 - axis_at))
    return gain


def noise(stream_key, dims, deviation, most, cuts=(), kind=jnp.bfloat16):
    factor_of = block_levels(stream_key, dims, cuts, -0.22, 0.18) if cuts else 1.0
    entries = jax.random.normal(stream_key, dims, jnp.float32) * deviation * factor_of
    return jnp.minimum(jnp.maximum(entries, -most), most).astype(kind)


def setup_inputs(seed: int = 0, part: int = 0) -> dict:
    key_list = jax.random.split(jax.random.key(seed), 6)
    part_splits = jax.random.split(jax.random.fold_in(key_list[5], part), 6)
    return {
        "spectra": noise(part_splits[0], (S_TOTAL, W), 1.0, 6.0, ((0, 16),), jnp.float32),
        "offsets": draw_offsets(jax.random.fold_in(jax.random.fold_in(key_list[5], part), 71), part),
        "mask_bits": with_ends(jax.random.randint(part_splits[2], (S_TOTAL, W // 16), 0, 65536), jax.random.fold_in(part_splits[2], 1), 0, 65535).astype(jnp.int32),
        "eigen": draw_eigen(jax.random.fold_in(key_list[5], 71), part),
        "plan": draw_plan(jax.random.fold_in(jax.random.fold_in(key_list[5], part), 71), part),
    }


def unpack_bits(words):
    shifts = jnp.arange(16, dtype=jnp.int32)
    bits = jnp.right_shift(words[..., None], shifts) & 1
    return bits.reshape(words.shape[0], -1).astype(jnp.float32)

def place_rows(rows, shifts, length):

    def place_one(row, start):
        return lax.dynamic_update_slice(jnp.zeros((length,), rows.dtype), row, (start,))
    return jax.vmap(place_one)(rows, shifts)

def take_rows(rows, shifts, width):

    def take_one(row, start):
        return lax.dynamic_slice(row, (start,), (width,))
    return jax.vmap(take_one)(rows, shifts)

def process_block(table, flux, starts, words, length):
    width = flux.shape[1]
    pixels = table.shape[1]
    scale = 1.0 / math.sqrt(width)
    starts = starts.astype(jnp.int32)
    first = jnp.clip(jnp.min(starts), 0, pixels - length).astype(jnp.int32)
    window = lax.dynamic_slice_in_dim(table, first, length, 1)
    shifted = (starts - first).astype(jnp.int32)
    goodness = unpack_bits(words)
    masked = place_rows(goodness * flux, shifted, length)
    coef = jnp.dot(masked, window.T, precision=lax.Precision.HIGHEST) * scale
    fitted_window = jnp.dot(coef, window, precision=lax.Precision.HIGHEST) * scale
    fitted = take_rows(fitted_window, shifted, width)
    resid = goodness * (flux - fitted)
    weighted = resid / (1.0 + resid * resid)
    placed = place_rows(weighted, shifted, length)
    grad_window = jnp.dot(coef.T, placed, precision=lax.Precision.HIGHEST)
    return (coef, first, grad_window)

def reference(spectra, offsets, mask_bits, eigen, plan):
    length = min(P_SIZE, W + SPAN + (P_SIZE - W - SPAN) // (NB * N_GZ) + 4)

    def step(grad, blocks):
        flux, starts, words = blocks
        coef, first, grad_window = process_block(eigen, flux, starts, words, length)
        current = lax.dynamic_slice_in_dim(grad, first, length, 1)
        grad = lax.dynamic_update_slice_in_dim(grad, current + grad_window, first, 1)
        return (grad, coef)
    flux_blocks = spectra.reshape(-1, BS, W)
    start_blocks = offsets.reshape(-1, BS)
    word_blocks = mask_bits.reshape(-1, BS, W // 16)
    grad, coefs = lax.scan(step, jnp.zeros((K, P_SIZE), jnp.float32), (flux_blocks, start_blocks, word_blocks))
    eta = 2.0 / math.sqrt(S_TOTAL * W / P_SIZE)
    update = eigen + eta * grad
    eigen_new = update / jnp.sqrt(lax.optimization_barrier(jnp.mean(update * update, axis=1, keepdims=True)) + 1e-06)
    coef_all = coefs.reshape(N_GZ, NB, BS * K)
    output = jnp.concatenate([coef_all, jnp.zeros((N_GZ, 1, BS * K), jnp.float32)], axis=1)
    source = plan[:, 0].astype(jnp.int32)
    target = plan[:, 1].astype(jnp.int32)
    blocks = plan[:, 2].astype(jnp.int32)
    moved = coef_all[source, blocks]
    output = output.at[target, NB].set(moved)
    output = output.at[source, blocks].set(0.0)
    return (output, eigen_new)
```

```python
import functools
import math

import jax
import jax.numpy as jnp
from jax import lax
from jax.experimental import pallas as pl
from jax.experimental.pallas import tpu as pltpu
from jax.sharding import PartitionSpec as P

NB = 4
BS = 16
SPAN = 128
LANES = 128
TILE = 256


class Geometry:
    def __init__(self, devices, rows, width, pixels, rank):
        self.devices, self.rows, self.width = devices, rows, width
        self.pixels, self.rank = pixels, rank
        self.total = devices * rows
        self.ramp = pixels - width - SPAN
        per_block = ((BS - 1) * self.ramp) // self.total + 1
        self.reach = -(-(per_block + SPAN + LANES - 1) // LANES)
        self.sub = width // LANES + self.reach
        lead = (((NB - 1) * BS * self.ramp) // self.total + LANES) // LANES
        win = self.sub + lead
        self.win = win + win % 2
        self.window = self.win * LANES
        self.scale = 1.0 / math.sqrt(width)
        self.eta = 2.0 / math.sqrt(self.total * width / pixels)

    def aligned(self, spectrum, chunks):
        start = lax.div(lax.div(spectrum * self.ramp, self.total), LANES)
        return jnp.minimum(start, self.pixels // LANES - chunks)

    def device_chunk(self, device):
        return self.aligned(device * self.rows, self.win)

    def block_chunk(self, device, block):
        return self.aligned(device * self.rows + block * BS, self.sub)


def split(x):
    high = x.astype(jnp.bfloat16)
    low = (x - high.astype(jnp.float32)).astype(jnp.bfloat16)
    return high, low


def columns(chunk, count=1):
    return pl.ds(pl.multiple_of(chunk * LANES, LANES), count * LANES)


def lane_take(x, index):
    return jnp.take_along_axis(x, index, axis=1, mode="promise_in_bounds")


def place(geo, me, flux_ref, off_ref, word_ref, pf, pm, phl):
    edge = max(geo.win - geo.sub, 1)
    for lo in (0, geo.win - edge):
        cols = pl.ds(lo * LANES, edge * LANES)
        pf[:, cols] = jnp.zeros((geo.rows, edge * LANES), jnp.float32)
        pm[:, cols] = jnp.zeros((geo.rows, edge * LANES), jnp.float32)
        phl[:, cols] = jnp.zeros((2 * geo.rows, edge * LANES), jnp.bfloat16)
    device_chunk = geo.device_chunk(me)
    lane = lax.broadcasted_iota(jnp.int32, (BS, LANES), 1)
    row = lax.broadcasted_iota(jnp.int32, (BS, LANES), 0)
    flux_chunks = geo.width // LANES

    def body(block, carry):
        first = geo.block_chunk(me, block)
        delta = first - device_chunk
        base = pl.multiple_of(block * BS, BS)
        offs = jnp.zeros((BS, LANES), jnp.int32)
        for s in range(BS):
            offs = jnp.where(row == s, off_ref[base + s], offs)
        u = lane - (offs - first * LANES)
        back = lax.shift_right_arithmetic(u, 7)
        lane_index = u & (LANES - 1)
        bit = u & 15
        word = lax.shift_right_arithmetic(u, 4)
        picks = [back == -d for d in range(geo.reach)]
        zero = jnp.zeros((BS, LANES), jnp.float32)
        words = [
            word_ref[pl.ds(base, BS), pl.ds(i * LANES, LANES)]
            for i in range(geo.width // 16 // LANES)
        ]
        per_word = 16 * LANES
        taken = {}
        for c in range(geo.sub):
            if c < flux_chunks:
                taken[c] = lane_take(
                    flux_ref[pl.ds(base, BS), pl.ds(c * LANES, LANES)], lane_index
                )
            value = taken.get(c - geo.reach, zero)
            for d in reversed(range(geo.reach)):
                value = jnp.where(picks[d], taken.get(c - d, zero), value)
            taken.pop(c - geo.reach, None)
            index = (word + 8 * c) & (LANES - 1)
            lowest = max((c - geo.reach) * LANES, 0)
            highest = min(c * LANES + LANES - 1, geo.width - 1)
            first_word, last_word = lowest // per_word, highest // per_word
            bits = lane_take(words[first_word], index)
            for w in range(first_word + 1, last_word + 1):
                later = u >= w * per_word - c * LANES
                bits = jnp.where(later, lane_take(words[w], index), bits)
            bits = lax.shift_right_logical(bits, bit) & 1
            if c < geo.reach:
                bits = jnp.where(u >= -c * LANES, bits, 0)
            if c >= flux_chunks:
                bits = jnp.where(u < geo.width - c * LANES, bits, 0)
            good = bits.astype(jnp.float32)
            value = value * good
            high, low = split(value)
            cols = columns(delta + c)
            pf[pl.ds(base, BS), cols] = value
            pm[pl.ds(base, BS), cols] = good
            phl[pl.ds(base, BS), cols] = high
            phl[pl.ds(geo.rows + base, BS), cols] = low
        return carry

    lax.fori_loop(0, NB, body, 0)


def solve(geo, me, table, pf, pm, phl, est, grad):
    rank, rows = geo.rank, geo.rows
    start = geo.device_chunk(me)
    step = TILE // LANES
    tiles = geo.win // step
    for t in range(tiles):
        high, low = split(table[:, columns(start + t * step, step)])
        cols = pl.ds(t * TILE, TILE)
        est[pl.ds(0, rank), cols] = high
        est[pl.ds(rank, rank), cols] = low
        est[pl.ds(2 * rank, rank), cols] = high
    both = lax.dot_general(
        phl[...],
        est[pl.ds(0, 2 * rank), :],
        (((1,), (1,)), ((), ())),
        preferred_element_type=jnp.float32,
    )
    both = both[:rows] + both[rows:]
    coef = (both[:, :rank] + both[:, rank:]) * geo.scale
    high, low = split(coef * geo.scale)
    high, low = high.astype(jnp.float32), low.astype(jnp.float32)
    left = jnp.concatenate([high, high, low], axis=1).astype(jnp.bfloat16)
    padded = jnp.concatenate([coef, jnp.zeros((rows, LANES - rank), jnp.float32)], axis=1)
    high, low = split(padded.T[:rank])
    high, low = high.astype(jnp.float32), low.astype(jnp.float32)
    across = jnp.concatenate([high, high, low], axis=1).astype(jnp.bfloat16)
    for t in range(tiles):
        cols = pl.ds(t * TILE, TILE)
        fit = jnp.dot(left, est[:, cols], preferred_element_type=jnp.float32)
        resid = pf[:, cols] - pm[:, cols] * fit
        weighted = resid / (1.0 + resid * resid)
        high, low = split(weighted)
        stack = jnp.concatenate([high, low, high], axis=0)
        grad[:, columns(start + t * step, step)] = jnp.dot(
            across, stack, preferred_element_type=jnp.float32
        )
    return coef


def plain_kernel(geo, flux_ref, off_ref, word_ref, table_ref, coef_ref, grad_ref, pf, pm, phl, est):
    me = lax.axis_index("gz")
    grad_ref[...] = jnp.zeros_like(grad_ref)
    place(geo, me, flux_ref, off_ref, word_ref, pf, pm, phl)
    coef_ref[...] = solve(geo, me, table_ref, pf, pm, phl, est, grad_ref)


def window_scratch(geo):
    return [
        pltpu.VMEM((geo.rows, geo.window), jnp.float32),
        pltpu.VMEM((geo.rows, geo.window), jnp.float32),
        pltpu.VMEM((2 * geo.rows, geo.window), jnp.bfloat16),
        pltpu.VMEM((3 * geo.rank, geo.window), jnp.bfloat16),
    ]


def plain(geo, spectra, offsets, mask_bits, eigen, plan):
    me = lax.axis_index("gz")
    table = lax.all_gather(eigen, "gz", axis=1, tiled=True)
    vmem = pl.BlockSpec(memory_space=pltpu.VMEM)
    smem = pl.BlockSpec(memory_space=pltpu.SMEM)
    coef, grad = pl.pallas_call(
        functools.partial(plain_kernel, geo),
        out_shape=(
            jax.ShapeDtypeStruct((geo.rows, geo.rank), jnp.float32),
            jax.ShapeDtypeStruct((geo.rank, geo.pixels), jnp.float32),
        ),
        in_specs=[vmem, smem, vmem, vmem],
        out_specs=(vmem, vmem),
        scratch_shapes=window_scratch(geo),
        compiler_params=pltpu.CompilerParams(vmem_limit_bytes=40 << 20),
    )(spectra, offsets, mask_bits, table)
    half = plan.shape[0]
    row = lax.dynamic_index_in_dim(plan, me % half, 0, keepdims=False)
    source, block = row[0] == me, row[2]
    blocks = coef.reshape(NB, BS * geo.rank)
    sent = lax.dynamic_index_in_dim(blocks, block, 0, keepdims=True)
    pairs = [(i, (i + half) % geo.devices) for i in range(geo.devices)]
    got = lax.ppermute(sent, "gz", pairs)
    own = jnp.arange(NB, dtype=jnp.int32)[:, None] == block
    blocks = jnp.where(source & own, 0.0, blocks)
    got = jnp.where(source, 0.0, got)
    coefficients = jnp.concatenate([blocks, got], axis=0)[None]
    mine = lax.psum_scatter(grad, "gz", scatter_dimension=1, tiled=True)
    update = eigen + geo.eta * mine
    squares = lax.psum(jnp.sum(update * update, axis=1), "gz")
    eigen_new = update / jnp.sqrt(squares[:, None] / geo.pixels + 1e-06)
    return coefficients, eigen_new


def local(spectra, offsets, mask_bits, eigen, plan):
    devices = lax.axis_size("gz")
    rank, shard = eigen.shape
    geo = Geometry(devices, spectra.shape[0], spectra.shape[1], shard * devices, rank)
    return plain(geo, spectra, offsets, mask_bits, eigen, plan)


def solution(mesh):
    placed = (
        P(("grp", "gz"), None),
        P(("grp", "gz")),
        P(("grp", "gz"), None),
        P(None, "gz"),
        P("grp", None),
    )
    return jax.shard_map(
        local,
        mesh=mesh,
        in_specs=placed,
        out_specs=(P(("grp", "gz"), None, None), P("grp", "gz")),
        check_vma=False,
    )
```

```python
import functools
import math

import jax
import jax.numpy as jnp
from jax import lax
from jax.experimental import pallas as pl
from jax.experimental.pallas import tpu as pltpu
from jax.sharding import PartitionSpec as P

NB = 4
BS = 16
SPAN = 128
LANES = 128
TILE = 256


class Geometry:
    def __init__(self, devices, rows, width, pixels, rank):
        self.devices, self.rows, self.width = devices, rows, width
        self.pixels, self.rank = pixels, rank
        self.total = devices * rows
        self.ramp = pixels - width - SPAN
        per_block = ((BS - 1) * self.ramp) // self.total + 1
        self.reach = -(-(per_block + SPAN + LANES - 1) // LANES)
        self.sub = width // LANES + self.reach
        lead = (((NB - 1) * BS * self.ramp) // self.total + LANES) // LANES
        win = self.sub + lead
        self.win = win + win % 2
        self.window = self.win * LANES
        self.scale = 1.0 / math.sqrt(width)
        self.eta = 2.0 / math.sqrt(self.total * width / pixels)

    def aligned(self, spectrum, chunks):
        start = lax.div(lax.div(spectrum * self.ramp, self.total), LANES)
        return jnp.minimum(start, self.pixels // LANES - chunks)

    def device_chunk(self, device):
        return self.aligned(device * self.rows, self.win)

    def block_chunk(self, device, block):
        return self.aligned(device * self.rows + block * BS, self.sub)


def split(x):
    high = x.astype(jnp.bfloat16)
    low = (x - high.astype(jnp.float32)).astype(jnp.bfloat16)
    return high, low


def columns(chunk, count=1):
    return pl.ds(pl.multiple_of(chunk * LANES, LANES), count * LANES)


def lane_take(x, index):
    return jnp.take_along_axis(x, index, axis=1, mode="promise_in_bounds")


def place(geo, me, flux_ref, off_ref, word_ref, pf, pm, phl):
    edge = max(geo.win - geo.sub, 1)
    for lo in (0, geo.win - edge):
        cols = pl.ds(lo * LANES, edge * LANES)
        pf[:, cols] = jnp.zeros((geo.rows, edge * LANES), jnp.float32)
        pm[:, cols] = jnp.zeros((geo.rows, edge * LANES), jnp.float32)
        phl[:, cols] = jnp.zeros((2 * geo.rows, edge * LANES), jnp.bfloat16)
    device_chunk = geo.device_chunk(me)
    lane = lax.broadcasted_iota(jnp.int32, (BS, LANES), 1)
    row = lax.broadcasted_iota(jnp.int32, (BS, LANES), 0)
    flux_chunks = geo.width // LANES

    def body(block, carry):
        first = geo.block_chunk(me, block)
        delta = first - device_chunk
        base = pl.multiple_of(block * BS, BS)
        offs = jnp.zeros((BS, LANES), jnp.int32)
        for s in range(BS):
            offs = jnp.where(row == s, off_ref[base + s], offs)
        u = lane - (offs - first * LANES)
        back = lax.shift_right_arithmetic(u, 7)
        lane_index = u & (LANES - 1)
        bit = u & 15
        word = lax.shift_right_arithmetic(u, 4)
        picks = [back == -d for d in range(geo.reach)]
        zero = jnp.zeros((BS, LANES), jnp.float32)
        words = [
            word_ref[pl.ds(base, BS), pl.ds(i * LANES, LANES)]
            for i in range(geo.width // 16 // LANES)
        ]
        per_word = 16 * LANES
        taken = {}
        for c in range(geo.sub):
            if c < flux_chunks:
                taken[c] = lane_take(
                    flux_ref[pl.ds(base, BS), pl.ds(c * LANES, LANES)], lane_index
                )
            value = taken.get(c - geo.reach, zero)
            for d in reversed(range(geo.reach)):
                value = jnp.where(picks[d], taken.get(c - d, zero), value)
            taken.pop(c - geo.reach, None)
            index = (word + 8 * c) & (LANES - 1)
            lowest = max((c - geo.reach) * LANES, 0)
            highest = min(c * LANES + LANES - 1, geo.width - 1)
            first_word, last_word = lowest // per_word, highest // per_word
            bits = lane_take(words[first_word], index)
            for w in range(first_word + 1, last_word + 1):
                later = u >= w * per_word - c * LANES
                bits = jnp.where(later, lane_take(words[w], index), bits)
            bits = lax.shift_right_logical(bits, bit) & 1
            if c < geo.reach:
                bits = jnp.where(u >= -c * LANES, bits, 0)
            if c >= flux_chunks:
                bits = jnp.where(u < geo.width - c * LANES, bits, 0)
            good = bits.astype(jnp.float32)
            value = value * good
            high, low = split(value)
            cols = columns(delta + c)
            pf[pl.ds(base, BS), cols] = value
            pm[pl.ds(base, BS), cols] = good
            phl[pl.ds(base, BS), cols] = high
            phl[pl.ds(geo.rows + base, BS), cols] = low
        return carry

    lax.fori_loop(0, NB, body, 0)


def solve(geo, me, table, pf, pm, phl, est, grad):
    rank, rows = geo.rank, geo.rows
    start = geo.device_chunk(me)
    step = TILE // LANES
    tiles = geo.win // step
    for t in range(tiles):
        high, low = split(table[:, columns(start + t * step, step)])
        cols = pl.ds(t * TILE, TILE)
        est[pl.ds(0, rank), cols] = high
        est[pl.ds(rank, rank), cols] = low
        est[pl.ds(2 * rank, rank), cols] = high
    both = lax.dot_general(
        phl[...],
        est[pl.ds(0, 2 * rank), :],
        (((1,), (1,)), ((), ())),
        preferred_element_type=jnp.float32,
    )
    both = both[:rows] + both[rows:]
    coef = (both[:, :rank] + both[:, rank:]) * geo.scale
    high, low = split(coef * geo.scale)
    high, low = high.astype(jnp.float32), low.astype(jnp.float32)
    left = jnp.concatenate([high, high, low], axis=1).astype(jnp.bfloat16)
    padded = jnp.concatenate([coef, jnp.zeros((rows, LANES - rank), jnp.float32)], axis=1)
    high, low = split(padded.T[:rank])
    high, low = high.astype(jnp.float32), low.astype(jnp.float32)
    across = jnp.concatenate([high, high, low], axis=1).astype(jnp.bfloat16)
    for t in range(tiles):
        cols = pl.ds(t * TILE, TILE)
        fit = jnp.dot(left, est[:, cols], preferred_element_type=jnp.float32)
        resid = pf[:, cols] - pm[:, cols] * fit
        weighted = resid / (1.0 + resid * resid)
        high, low = split(weighted)
        stack = jnp.concatenate([high, low, high], axis=0)
        grad[:, columns(start + t * step, step)] = jnp.dot(
            across, stack, preferred_element_type=jnp.float32
        )
    return coef


def plain_kernel(geo, flux_ref, off_ref, word_ref, table_ref, coef_ref, grad_ref, pf, pm, phl, est):
    me = lax.axis_index("gz")
    grad_ref[...] = jnp.zeros_like(grad_ref)
    place(geo, me, flux_ref, off_ref, word_ref, pf, pm, phl)
    coef_ref[...] = solve(geo, me, table_ref, pf, pm, phl, est, grad_ref)


def window_scratch(geo):
    return [
        pltpu.VMEM((geo.rows, geo.window), jnp.float32),
        pltpu.VMEM((geo.rows, geo.window), jnp.float32),
        pltpu.VMEM((2 * geo.rows, geo.window), jnp.bfloat16),
        pltpu.VMEM((3 * geo.rank, geo.window), jnp.bfloat16),
    ]


def plain(geo, spectra, offsets, mask_bits, eigen, plan):
    me = lax.axis_index("gz")
    table = lax.all_gather(eigen, "gz", axis=1, tiled=True)
    vmem = pl.BlockSpec(memory_space=pltpu.VMEM)
    smem = pl.BlockSpec(memory_space=pltpu.SMEM)
    coef, grad = pl.pallas_call(
        functools.partial(plain_kernel, geo),
        out_shape=(
            jax.ShapeDtypeStruct((geo.rows, geo.rank), jnp.float32),
            jax.ShapeDtypeStruct((geo.rank, geo.pixels), jnp.float32),
        ),
        in_specs=[vmem, smem, vmem, vmem],
        out_specs=(vmem, vmem),
        scratch_shapes=window_scratch(geo),
        compiler_params=pltpu.CompilerParams(vmem_limit_bytes=40 << 20),
    )(spectra, offsets, mask_bits, table)
    half = plan.shape[0]
    row = lax.dynamic_index_in_dim(plan, me % half, 0, keepdims=False)
    source, block = row[0] == me, row[2]
    blocks = coef.reshape(NB, BS * geo.rank)
    sent = lax.dynamic_index_in_dim(blocks, block, 0, keepdims=True)
    pairs = [(i, (i + half) % geo.devices) for i in range(geo.devices)]
    got = lax.ppermute(sent, "gz", pairs)
    own = jnp.arange(NB, dtype=jnp.int32)[:, None] == block
    blocks = jnp.where(source & own, 0.0, blocks)
    got = jnp.where(source, 0.0, got)
    coefficients = jnp.concatenate([blocks, got], axis=0)[None]
    mine = lax.psum_scatter(grad, "gz", scatter_dimension=1, tiled=True)
    update = eigen + geo.eta * mine
    squares = lax.psum(jnp.sum(update * update, axis=1), "gz")
    eigen_new = update / jnp.sqrt(squares[:, None] / geo.pixels + 1e-06)
    return coefficients, eigen_new


def fused_kernel(
    geo, half, flux_ref, off_ref, word_ref, eigen_ref, plan_ref, coef_ref, new_ref,
    pf, pm, phl, est, table, grad, incoming, row_out, row_in, coef_out, coef_in,
    table_sent, table_got, grad_sent, grad_got, row_sent, row_got, coef_sent, coef_got,
):
    me = lax.axis_index("gz")
    devices, rank, rows = geo.devices, geo.rank, geo.rows
    shard = geo.pixels // devices
    per = shard // LANES

    def needs(device, owner):
        first = geo.device_chunk(device)
        low = lax.div(first, per)
        high = lax.div(first + geo.win - 1, per)
        return jnp.logical_and(low <= owner, owner <= high)

    def peers(body):
        def step(k, carry):
            body(lax.rem(me + k, devices))
            return carry

        lax.fori_loop(1, devices, step, 0)

    def table_copy(peer, owner):
        return pltpu.make_async_remote_copy(
            src_ref=eigen_ref,
            dst_ref=table.at[:, columns(owner * per, per)],
            send_sem=table_sent.at[peer],
            recv_sem=table_got.at[owner],
            device_id={"gz": peer},
            device_id_type=pl.DeviceIdType.MESH,
        )

    def grad_copy(owner, source):
        return pltpu.make_async_remote_copy(
            src_ref=grad.at[:, columns(owner * per, per)],
            dst_ref=incoming.at[source],
            send_sem=grad_sent.at[owner],
            recv_sem=grad_got.at[source],
            device_id={"gz": owner},
            device_id_type=pl.DeviceIdType.MESH,
        )

    def row_copy(peer, source):
        return pltpu.make_async_remote_copy(
            src_ref=row_out,
            dst_ref=row_in.at[source],
            send_sem=row_sent.at[peer],
            recv_sem=row_got.at[source],
            device_id={"gz": peer},
            device_id_type=pl.DeviceIdType.MESH,
        )

    barrier = pltpu.get_barrier_semaphore()
    peers(lambda peer: pl.semaphore_signal(
        barrier, inc=1, device_id={"gz": peer}, device_id_type=pl.DeviceIdType.MESH
    ))
    pl.semaphore_wait(barrier, devices - 1)

    @peers
    def _(peer):
        @pl.when(needs(peer, me))
        def _():
            table_copy(peer, me).start()

    table[:, columns(me * per, per)] = eigen_ref[...]
    grad[...] = jnp.zeros_like(grad)
    place(geo, me, flux_ref, off_ref, word_ref, pf, pm, phl)

    @peers
    def _(peer):
        @pl.when(needs(me, peer))
        def _():
            table_copy(peer, peer).wait_recv()

    coef = solve(geo, me, table, pf, pm, phl, est, grad)

    @peers
    def _(peer):
        @pl.when(needs(me, peer))
        def _():
            grad_copy(peer, me).start()

    padded = jnp.concatenate([coef, jnp.zeros((rows, LANES - rank), jnp.float32)], axis=1)
    lane = lax.broadcasted_iota(jnp.int32, (BS, LANES), 1)
    row = lax.broadcasted_iota(jnp.int32, (BS, LANES), 0)
    plan_row = lax.rem(me, half)
    source, block = plan_ref[plan_row, 0], plan_ref[plan_row, 2]
    group = LANES // rank
    for h in range(BS // group):
        here = row == lax.div(lane, rank) + h * group
        cols = pl.ds(h * LANES, LANES)
        sent = jnp.zeros((1, LANES), jnp.float32)
        for b in range(NB):
            spread = lane_take(padded[b * BS:(b + 1) * BS], lane & (rank - 1))
            flat = jnp.sum(jnp.where(here, spread, 0.0), axis=0, keepdims=True)
            planned = jnp.where(block == b, 1.0, 0.0)
            gone = planned * jnp.where(source == me, 1.0, 0.0)
            sent = sent + flat * planned
            coef_ref[0, pl.ds(b, 1), cols] = flat * (1.0 - gone)
        coef_out[:, cols] = sent
    partner = lax.rem(me + half, devices)
    coef_copy = pltpu.make_async_remote_copy(
        src_ref=coef_out,
        dst_ref=coef_in,
        send_sem=coef_sent,
        recv_sem=coef_got,
        device_id={"gz": partner},
        device_id_type=pl.DeviceIdType.MESH,
    )
    coef_copy.start()

    new_ref[...] = grad[:, columns(me * per, per)]

    @peers
    def _(peer):
        @pl.when(needs(peer, me))
        def _():
            grad_copy(me, peer).wait_recv()
            new_ref[...] += incoming[peer]

    update = eigen_ref[...] + geo.eta * new_ref[...]
    new_ref[...] = update
    squares = jnp.sum(update * update, axis=1, keepdims=True)
    wide = lax.broadcasted_iota(jnp.int32, (rank, LANES), 1)
    tall = lax.broadcasted_iota(jnp.int32, (rank, LANES), 0)
    diagonal = wide == tall
    packed = jnp.sum(jnp.where(diagonal, squares, 0.0), axis=0, keepdims=True)
    row_out[...] = packed
    peers(lambda peer: row_copy(peer, me).start())
    coef_copy.wait()
    coef_ref[0, pl.ds(NB, 1), :] = coef_in[...] * jnp.where(source == me, 0.0, 1.0)
    row_in[me] = packed
    peers(lambda peer: row_copy(peer, peer).wait_recv())
    total = row_in[0]
    for d in range(1, devices):
        total = total + row_in[d]
    mean = jnp.sum(jnp.where(diagonal, total, 0.0), axis=1, keepdims=True) / geo.pixels
    new_ref[...] = new_ref[...] / jnp.sqrt(mean + 1e-06)

    @peers
    def _(peer):
        row_copy(peer, me).wait_send()

        @pl.when(needs(peer, me))
        def _():
            table_copy(peer, me).wait_send()

        @pl.when(needs(me, peer))
        def _():
            grad_copy(peer, me).wait_send()


def fused(geo, spectra, offsets, mask_bits, eigen, plan):
    vmem = pl.BlockSpec(memory_space=pltpu.VMEM)
    smem = pl.BlockSpec(memory_space=pltpu.SMEM)
    shard = geo.pixels // geo.devices
    width = BS * geo.rank
    many = pltpu.SemaphoreType.DMA((geo.devices,))
    one = pltpu.SemaphoreType.DMA
    return pl.pallas_call(
        functools.partial(fused_kernel, geo, plan.shape[0]),
        out_shape=(
            jax.ShapeDtypeStruct((1, NB + 1, width), jnp.float32),
            jax.ShapeDtypeStruct((geo.rank, shard), jnp.float32),
        ),
        in_specs=[vmem, smem, vmem, vmem, smem],
        out_specs=(vmem, vmem),
        scratch_shapes=window_scratch(geo) + [
            pltpu.VMEM((geo.rank, geo.pixels), jnp.float32),
            pltpu.VMEM((geo.rank, geo.pixels), jnp.float32),
            pltpu.VMEM((geo.devices, geo.rank, shard), jnp.float32),
            pltpu.VMEM((1, LANES), jnp.float32),
            pltpu.VMEM((geo.devices, 1, LANES), jnp.float32),
            pltpu.VMEM((1, width), jnp.float32),
            pltpu.VMEM((1, width), jnp.float32),
            many, many, many, many, many, many, one, one,
        ],
        compiler_params=pltpu.CompilerParams(
            vmem_limit_bytes=40 << 20, collective_id=0, has_side_effects=True
        ),
    )(spectra, offsets, mask_bits, eigen, plan)


def local(spectra, offsets, mask_bits, eigen, plan):
    devices = lax.axis_size("gz")
    rank, shard = eigen.shape
    geo = Geometry(devices, spectra.shape[0], spectra.shape[1], shard * devices, rank)
    if shard % LANES == 0:
        return fused(geo, spectra, offsets, mask_bits, eigen, plan)
    return plain(geo, spectra, offsets, mask_bits, eigen, plan)


def solution(mesh):
    placed = (
        P(("grp", "gz"), None),
        P(("grp", "gz")),
        P(("grp", "gz"), None),
        P(None, "gz"),
        P("grp", None),
    )
    return jax.shard_map(
        local,
        mesh=mesh,
        in_specs=placed,
        out_specs=(P(("grp", "gz"), None, None), P("grp", "gz")),
        check_vma=False,
    )
```

```python
import functools
import math

import jax
import jax.numpy as jnp
from jax import lax
from jax.experimental import pallas as pl
from jax.experimental.pallas import tpu as pltpu
from jax.sharding import PartitionSpec as P

NB = 4
BS = 16
SPAN = 128
LANES = 128
TILE = 256


class Geometry:
    def __init__(self, devices, rows, width, pixels, rank):
        self.devices, self.rows, self.width = devices, rows, width
        self.pixels, self.rank = pixels, rank
        self.total = devices * rows
        self.ramp = pixels - width - SPAN
        per_block = ((BS - 1) * self.ramp) // self.total + 1
        self.reach = -(-(per_block + SPAN + LANES - 1) // LANES)
        self.sub = width // LANES + self.reach
        lead = (((NB - 1) * BS * self.ramp) // self.total + LANES) // LANES
        win = self.sub + lead
        self.win = win + win % 2
        self.window = self.win * LANES
        self.scale = 1.0 / math.sqrt(width)
        self.eta = 2.0 / math.sqrt(self.total * width / pixels)

    def aligned(self, spectrum, chunks):
        start = lax.div(lax.div(spectrum * self.ramp, self.total), LANES)
        return jnp.minimum(start, self.pixels // LANES - chunks)

    def static_range(self, device):
        first = min(device * self.rows * self.ramp // self.total // LANES,
                    self.pixels // LANES - self.win)
        per = self.pixels // self.devices // LANES
        return first // per, (first + self.win - 1) // per

    def ranges(self, me):
        shards = [self.static_range(d) for d in range(self.devices)]
        low, high, first, last = 0, 0, 0, -1
        for d, (a, b) in enumerate(shards):
            low = jnp.where(me == d, a, low)
            high = jnp.where(me == d, b, high)
            first = first + jnp.where(me > b, 1, 0)
            last = last + jnp.where(me >= a, 1, 0)
        return low, high, first, last

    def device_chunk(self, device):
        return self.aligned(device * self.rows, self.win)

    def block_chunk(self, device, block):
        return self.aligned(device * self.rows + block * BS, self.sub)


def split(x):
    high = x.astype(jnp.bfloat16)
    low = (x - high.astype(jnp.float32)).astype(jnp.bfloat16)
    return high, low


def columns(chunk, count=1):
    return pl.ds(pl.multiple_of(chunk * LANES, LANES), count * LANES)


def lane_take(x, index):
    return jnp.take_along_axis(x, index, axis=1, mode="promise_in_bounds")


def place(geo, me, flux_ref, off_ref, word_ref, pf, pm, phl):
    edge = max(geo.win - geo.sub, 1)
    for lo in (0, geo.win - edge):
        cols = pl.ds(lo * LANES, edge * LANES)
        pf[:, cols] = jnp.zeros((geo.rows, edge * LANES), jnp.float32)
        pm[:, cols] = jnp.zeros((geo.rows, edge * LANES), jnp.float32)
        phl[:, cols] = jnp.zeros((2 * geo.rows, edge * LANES), jnp.bfloat16)
    device_chunk = geo.device_chunk(me)
    lane = lax.broadcasted_iota(jnp.int32, (BS, LANES), 1)
    row = lax.broadcasted_iota(jnp.int32, (BS, LANES), 0)
    flux_chunks = geo.width // LANES

    def body(block, carry):
        first = geo.block_chunk(me, block)
        delta = first - device_chunk
        base = pl.multiple_of(block * BS, BS)
        offs = jnp.zeros((BS, LANES), jnp.int32)
        for s in range(BS):
            offs = jnp.where(row == s, off_ref[base + s], offs)
        u = lane - (offs - first * LANES)
        back = lax.shift_right_arithmetic(u, 7)
        lane_index = u & (LANES - 1)
        bit = u & 15
        word = lax.shift_right_arithmetic(u, 4)
        picks = [back == -d for d in range(geo.reach)]
        zero = jnp.zeros((BS, LANES), jnp.float32)
        words = [
            word_ref[pl.ds(base, BS), pl.ds(i * LANES, LANES)]
            for i in range(geo.width // 16 // LANES)
        ]
        per_word = 16 * LANES
        taken = {}
        for c in range(geo.sub):
            if c < flux_chunks:
                taken[c] = lane_take(
                    flux_ref[pl.ds(base, BS), pl.ds(c * LANES, LANES)], lane_index
                )
            value = taken.get(c - geo.reach, zero)
            for d in reversed(range(geo.reach)):
                value = jnp.where(picks[d], taken.get(c - d, zero), value)
            taken.pop(c - geo.reach, None)
            index = (word + 8 * c) & (LANES - 1)
            lowest = max((c - geo.reach) * LANES, 0)
            highest = min(c * LANES + LANES - 1, geo.width - 1)
            first_word, last_word = lowest // per_word, highest // per_word
            bits = lane_take(words[first_word], index)
            for w in range(first_word + 1, last_word + 1):
                later = u >= w * per_word - c * LANES
                bits = jnp.where(later, lane_take(words[w], index), bits)
            bits = lax.shift_right_logical(bits, bit) & 1
            if c < geo.reach:
                bits = jnp.where(u >= -c * LANES, bits, 0)
            if c >= flux_chunks:
                bits = jnp.where(u < geo.width - c * LANES, bits, 0)
            good = bits.astype(jnp.float32)
            value = value * good
            high, low = split(value)
            cols = columns(delta + c)
            pf[pl.ds(base, BS), cols] = value
            pm[pl.ds(base, BS), cols] = good
            phl[pl.ds(base, BS), cols] = high
            phl[pl.ds(geo.rows + base, BS), cols] = low
        return carry

    lax.fori_loop(0, NB, body, 0)


def solve(geo, me, table, pf, pm, phl, est, grad, after=None):
    rank, rows = geo.rank, geo.rows
    start = geo.device_chunk(me)
    step = TILE // LANES
    tiles = geo.win // step
    for t in range(tiles):
        high, low = split(table[:, columns(start + t * step, step)])
        cols = pl.ds(t * TILE, TILE)
        est[pl.ds(0, rank), cols] = high
        est[pl.ds(rank, rank), cols] = low
        est[pl.ds(2 * rank, rank), cols] = high
    both = lax.dot_general(
        phl[...],
        est[pl.ds(0, 2 * rank), :],
        (((1,), (1,)), ((), ())),
        preferred_element_type=jnp.float32,
    )
    both = both[:rows] + both[rows:]
    coef = (both[:, :rank] + both[:, rank:]) * geo.scale
    high, low = split(coef * geo.scale)
    high, low = high.astype(jnp.float32), low.astype(jnp.float32)
    left = jnp.concatenate([high, high, low], axis=1).astype(jnp.bfloat16)
    padded = jnp.concatenate([coef, jnp.zeros((rows, LANES - rank), jnp.float32)], axis=1)
    high, low = split(padded.T[:rank])
    high, low = high.astype(jnp.float32), low.astype(jnp.float32)
    across = jnp.concatenate([high, high, low], axis=1).astype(jnp.bfloat16)
    for t in range(tiles):
        cols = pl.ds(t * TILE, TILE)
        fit = jnp.dot(left, est[:, cols], preferred_element_type=jnp.float32)
        resid = pf[:, cols] - pm[:, cols] * fit
        weighted = resid / (1.0 + resid * resid)
        high, low = split(weighted)
        stack = jnp.concatenate([high, low, high], axis=0)
        grad[:, columns(start + t * step, step)] = jnp.dot(
            across, stack, preferred_element_type=jnp.float32
        )
        if after is not None and (t + 1 == tiles or t % 5 == 4):
            after(start + (t + 1) * step, t + 1 == tiles)
    return coef


def plain_kernel(geo, flux_ref, off_ref, word_ref, table_ref, coef_ref, grad_ref, pf, pm, phl, est):
    me = lax.axis_index("gz")
    grad_ref[...] = jnp.zeros_like(grad_ref)
    place(geo, me, flux_ref, off_ref, word_ref, pf, pm, phl)
    coef_ref[...] = solve(geo, me, table_ref, pf, pm, phl, est, grad_ref)


def window_scratch(geo):
    return [
        pltpu.VMEM((geo.rows, geo.window), jnp.float32),
        pltpu.VMEM((geo.rows, geo.window), jnp.float32),
        pltpu.VMEM((2 * geo.rows, geo.window), jnp.bfloat16),
        pltpu.VMEM((3 * geo.rank, geo.window), jnp.bfloat16),
    ]


def plain(geo, spectra, offsets, mask_bits, eigen, plan):
    me = lax.axis_index("gz")
    table = lax.all_gather(eigen, "gz", axis=1, tiled=True)
    vmem = pl.BlockSpec(memory_space=pltpu.VMEM)
    smem = pl.BlockSpec(memory_space=pltpu.SMEM)
    coef, grad = pl.pallas_call(
        functools.partial(plain_kernel, geo),
        out_shape=(
            jax.ShapeDtypeStruct((geo.rows, geo.rank), jnp.float32),
            jax.ShapeDtypeStruct((geo.rank, geo.pixels), jnp.float32),
        ),
        in_specs=[vmem, smem, vmem, vmem],
        out_specs=(vmem, vmem),
        scratch_shapes=window_scratch(geo),
        compiler_params=pltpu.CompilerParams(vmem_limit_bytes=40 << 20),
    )(spectra, offsets, mask_bits, table)
    half = plan.shape[0]
    row = lax.dynamic_index_in_dim(plan, me % half, 0, keepdims=False)
    source, block = row[0] == me, row[2]
    blocks = coef.reshape(NB, BS * geo.rank)
    sent = lax.dynamic_index_in_dim(blocks, block, 0, keepdims=True)
    pairs = [(i, (i + half) % geo.devices) for i in range(geo.devices)]
    got = lax.ppermute(sent, "gz", pairs)
    own = jnp.arange(NB, dtype=jnp.int32)[:, None] == block
    blocks = jnp.where(source & own, 0.0, blocks)
    got = jnp.where(source, 0.0, got)
    coefficients = jnp.concatenate([blocks, got], axis=0)[None]
    mine = lax.psum_scatter(grad, "gz", scatter_dimension=1, tiled=True)
    update = eigen + geo.eta * mine
    squares = lax.psum(jnp.sum(update * update, axis=1), "gz")
    eigen_new = update / jnp.sqrt(squares[:, None] / geo.pixels + 1e-06)
    return coefficients, eigen_new


def fused_kernel(
    geo, half, flux_hbm, off_ref, word_hbm, eigen_hbm, plan_ref, coef_ref, new_ref,
    pf, pm, phl, est, flux_ref, word_ref, table, grad, incoming,
    row_out, row_in, coef_out, coef_in, local_done,
    table_sent, table_got, grad_sent, grad_got, row_sent, row_got, coef_sent, coef_got,
):
    me = lax.axis_index("gz")
    devices, rank, rows = geo.devices, geo.rank, geo.rows
    shard = geo.pixels // devices
    per = shard // LANES
    low, high, first, last = geo.ranges(me)

    def peers(body):
        def step(k, carry):
            body(lax.rem(me + k, devices))
            return carry

        lax.fori_loop(1, devices, step, 0)

    def others(start, stop, body):
        def step(k, carry):
            @pl.when(k != me)
            def _():
                body(k)

            return carry

        lax.fori_loop(start, stop, step, 0)

    def table_copy(peer, owner):
        return pltpu.make_async_remote_copy(
            src_ref=eigen_hbm,
            dst_ref=table.at[:, columns(owner * per, per)],
            send_sem=table_sent.at[peer],
            recv_sem=table_got.at[owner],
            device_id={"gz": peer},
            device_id_type=pl.DeviceIdType.MESH,
        )

    def grad_copy(owner, source):
        return pltpu.make_async_remote_copy(
            src_ref=grad.at[:, columns(owner * per, per)],
            dst_ref=incoming.at[source],
            send_sem=grad_sent.at[owner],
            recv_sem=grad_got.at[source],
            device_id={"gz": owner},
            device_id_type=pl.DeviceIdType.MESH,
        )

    def row_copy(peer, source):
        return pltpu.make_async_remote_copy(
            src_ref=row_out,
            dst_ref=row_in.at[source],
            send_sem=row_sent.at[peer],
            recv_sem=row_got.at[source],
            device_id={"gz": peer},
            device_id_type=pl.DeviceIdType.MESH,
        )

    copies = [
        pltpu.make_async_copy(flux_hbm, flux_ref, local_done.at[0]),
        pltpu.make_async_copy(word_hbm, word_ref, local_done.at[1]),
        pltpu.make_async_copy(eigen_hbm, table.at[:, columns(me * per, per)], local_done.at[2]),
    ]
    for copy in copies:
        copy.start()
    barrier = pltpu.get_barrier_semaphore()
    peers(lambda peer: pl.semaphore_signal(
        barrier, inc=1, device_id={"gz": peer}, device_id_type=pl.DeviceIdType.MESH
    ))
    pl.semaphore_wait(barrier, devices - 1)
    others(first, last + 1, lambda peer: table_copy(peer, me).start())
    grad[...] = jnp.zeros_like(grad)
    copies[0].wait()
    copies[1].wait()
    place(geo, me, flux_ref, off_ref, word_ref, pf, pm, phl)
    copies[2].wait()
    others(low, high + 1, lambda owner: table_copy(owner, owner).wait_recv())
    begun = [low]

    def after(chunk, done):
        stop = high + 1 if done else lax.div(chunk, per)
        others(begun[0], stop, lambda owner: grad_copy(owner, me).start())
        begun[0] = stop

    coef = solve(geo, me, table, pf, pm, phl, est, grad, after)

    padded = jnp.concatenate([coef, jnp.zeros((rows, LANES - rank), jnp.float32)], axis=1)
    lane = lax.broadcasted_iota(jnp.int32, (BS, LANES), 1)
    row = lax.broadcasted_iota(jnp.int32, (BS, LANES), 0)
    plan_row = lax.rem(me, half)
    source, block = plan_ref[0, plan_row], plan_ref[2, plan_row]
    group = LANES // rank
    for h in range(BS // group):
        here = row == lax.div(lane, rank) + h * group
        cols = pl.ds(h * LANES, LANES)
        sent = jnp.zeros((1, LANES), jnp.float32)
        for b in range(NB):
            spread = lane_take(padded[b * BS:(b + 1) * BS], lane & (rank - 1))
            flat = jnp.sum(jnp.where(here, spread, 0.0), axis=0, keepdims=True)
            planned = jnp.where(block == b, 1.0, 0.0)
            gone = planned * jnp.where(source == me, 1.0, 0.0)
            sent = sent + flat * planned
            coef_ref[0, pl.ds(b, 1), cols] = flat * (1.0 - gone)
        coef_out[:, cols] = sent
    partner = lax.rem(me + half, devices)
    coef_copy = pltpu.make_async_remote_copy(
        src_ref=coef_out,
        dst_ref=coef_in,
        send_sem=coef_sent,
        recv_sem=coef_got,
        device_id={"gz": partner},
        device_id_type=pl.DeviceIdType.MESH,
    )
    coef_copy.start()

    new_ref[...] = grad[:, columns(me * per, per)]

    def add(peer):
        grad_copy(me, peer).wait_recv()
        new_ref[...] += incoming[peer]

    others(first, last + 1, add)
    update = table[:, columns(me * per, per)] + geo.eta * new_ref[...]
    new_ref[...] = update
    squares = jnp.sum(update * update, axis=1, keepdims=True)
    wide = lax.broadcasted_iota(jnp.int32, (rank, LANES), 1)
    tall = lax.broadcasted_iota(jnp.int32, (rank, LANES), 0)
    diagonal = wide == tall
    packed = jnp.sum(jnp.where(diagonal, squares, 0.0), axis=0, keepdims=True)
    row_out[...] = packed
    peers(lambda peer: row_copy(peer, me).start())
    coef_copy.wait()
    coef_ref[0, pl.ds(NB, 1), :] = coef_in[...] * jnp.where(source == me, 0.0, 1.0)
    row_in[me] = packed
    peers(lambda peer: row_copy(peer, peer).wait_recv())
    total = row_in[0]
    for d in range(1, devices):
        total = total + row_in[d]
    mean = jnp.sum(jnp.where(diagonal, total, 0.0), axis=1, keepdims=True) / geo.pixels
    new_ref[...] = new_ref[...] / jnp.sqrt(mean + 1e-06)

    peers(lambda peer: row_copy(peer, me).wait_send())
    others(first, last + 1, lambda peer: table_copy(peer, me).wait_send())
    others(low, high + 1, lambda owner: grad_copy(owner, me).wait_send())


def fused(geo, spectra, offsets, mask_bits, eigen, plan):
    vmem = pl.BlockSpec(memory_space=pltpu.VMEM)
    smem = pl.BlockSpec(memory_space=pltpu.SMEM)
    hbm = pl.BlockSpec(memory_space=pltpu.HBM)
    shard = geo.pixels // geo.devices
    width = BS * geo.rank
    many = pltpu.SemaphoreType.DMA((geo.devices,))
    one = pltpu.SemaphoreType.DMA
    return pl.pallas_call(
        functools.partial(fused_kernel, geo, plan.shape[0]),
        out_shape=(
            jax.ShapeDtypeStruct((1, NB + 1, width), jnp.float32),
            jax.ShapeDtypeStruct((geo.rank, shard), jnp.float32),
        ),
        in_specs=[hbm, smem, hbm, hbm, smem],
        out_specs=(vmem, vmem),
        scratch_shapes=window_scratch(geo) + [
            pltpu.VMEM(spectra.shape, jnp.float32),
            pltpu.VMEM(mask_bits.shape, jnp.int32),
            pltpu.VMEM((geo.rank, geo.pixels), jnp.float32),
            pltpu.VMEM((geo.rank, geo.pixels), jnp.float32),
            pltpu.VMEM((geo.devices, geo.rank, shard), jnp.float32),
            pltpu.VMEM((1, LANES), jnp.float32),
            pltpu.VMEM((geo.devices, 1, LANES), jnp.float32),
            pltpu.VMEM((1, width), jnp.float32),
            pltpu.VMEM((1, width), jnp.float32),
            pltpu.SemaphoreType.DMA((3,)),
            many, many, many, many, many, many, one, one,
        ],
        compiler_params=pltpu.CompilerParams(
            vmem_limit_bytes=64 << 20, collective_id=0, has_side_effects=True
        ),
    )(spectra, offsets, mask_bits, eigen, plan.T)


def local(spectra, offsets, mask_bits, eigen, plan):
    devices = lax.axis_size("gz")
    rank, shard = eigen.shape
    geo = Geometry(devices, spectra.shape[0], spectra.shape[1], shard * devices, rank)
    if shard % LANES == 0:
        return fused(geo, spectra, offsets, mask_bits, eigen, plan)
    return plain(geo, spectra, offsets, mask_bits, eigen, plan)


def solution(mesh):
    placed = (
        P(("grp", "gz"), None),
        P(("grp", "gz")),
        P(("grp", "gz"), None),
        P(None, "gz"),
        P("grp", None),
    )
    return jax.shard_map(
        local,
        mesh=mesh,
        in_specs=placed,
        out_specs=(P(("grp", "gz"), None, None), P("grp", "gz")),
        check_vma=False,
    )
```

```python
import functools
import math

import jax
import jax.numpy as jnp
from jax import lax
from jax.experimental import pallas as pl
from jax.experimental.pallas import tpu as pltpu
from jax.sharding import PartitionSpec as P

NB = 4
BS = 16
SPAN = 128
LANES = 128
TILE = 256


class Geometry:
    def __init__(self, devices, rows, width, pixels, rank):
        self.devices, self.rows, self.width = devices, rows, width
        self.pixels, self.rank = pixels, rank
        self.total = devices * rows
        self.ramp = pixels - width - SPAN
        per_block = ((BS - 1) * self.ramp) // self.total + 1
        self.reach = -(-(per_block + SPAN + LANES - 1) // LANES)
        self.sub = width // LANES + self.reach
        lead = (((NB - 1) * BS * self.ramp) // self.total + LANES) // LANES
        win = self.sub + lead
        self.win = win + win % 2
        self.window = self.win * LANES
        self.scale = 1.0 / math.sqrt(width)
        self.eta = 2.0 / math.sqrt(self.total * width / pixels)

    def aligned(self, spectrum, chunks):
        start = lax.div(lax.div(spectrum * self.ramp, self.total), LANES)
        return jnp.minimum(start, self.pixels // LANES - chunks)

    def static_range(self, device):
        first = min(device * self.rows * self.ramp // self.total // LANES,
                    self.pixels // LANES - self.win)
        per = self.pixels // self.devices // LANES
        return first // per, (first + self.win - 1) // per

    def ranges(self, me):
        shards = [self.static_range(d) for d in range(self.devices)]
        low, high, first, last = 0, 0, 0, -1
        for d, (a, b) in enumerate(shards):
            low = jnp.where(me == d, a, low)
            high = jnp.where(me == d, b, high)
            first = first + jnp.where(me > b, 1, 0)
            last = last + jnp.where(me >= a, 1, 0)
        return low, high, first, last

    def device_chunk(self, device):
        return self.aligned(device * self.rows, self.win)

    def block_chunk(self, device, block):
        return self.aligned(device * self.rows + block * BS, self.sub)


def split(x):
    high = x.astype(jnp.bfloat16)
    low = (x - high.astype(jnp.float32)).astype(jnp.bfloat16)
    return high, low


def columns(chunk, count=1):
    return pl.ds(pl.multiple_of(chunk * LANES, LANES), count * LANES)


def lane_take(x, index):
    return jnp.take_along_axis(x, index, axis=1, mode="promise_in_bounds")


def place(geo, me, flux_ref, off_ref, word_ref, pf, pm, phl):
    edge = max(geo.win - geo.sub, 1)
    for lo in (0, geo.win - edge):
        cols = pl.ds(lo * LANES, edge * LANES)
        pf[:, cols] = jnp.zeros((geo.rows, edge * LANES), jnp.float32)
        pm[:, cols] = jnp.zeros((geo.rows, edge * LANES), jnp.float32)
        phl[:, cols] = jnp.zeros((2 * geo.rows, edge * LANES), jnp.bfloat16)
    device_chunk = geo.device_chunk(me)
    lane = lax.broadcasted_iota(jnp.int32, (BS, LANES), 1)
    row = lax.broadcasted_iota(jnp.int32, (BS, LANES), 0)
    flux_chunks = geo.width // LANES

    def body(block, carry):
        first = geo.block_chunk(me, block)
        delta = first - device_chunk
        base = pl.multiple_of(block * BS, BS)
        offs = jnp.zeros((BS, LANES), jnp.int32)
        for s in range(BS):
            offs = jnp.where(row == s, off_ref[base + s], offs)
        u = lane - (offs - first * LANES)
        back = lax.shift_right_arithmetic(u, 7)
        lane_index = u & (LANES - 1)
        bit = u & 15
        word = lax.shift_right_arithmetic(u, 4)
        picks = [back == -d for d in range(geo.reach)]
        zero = jnp.zeros((BS, LANES), jnp.float32)
        words = [
            word_ref[pl.ds(base, BS), pl.ds(i * LANES, LANES)]
            for i in range(geo.width // 16 // LANES)
        ]
        per_word = 16 * LANES
        taken = {}
        for c in range(geo.sub):
            if c < flux_chunks:
                taken[c] = lane_take(
                    flux_ref[pl.ds(base, BS), pl.ds(c * LANES, LANES)], lane_index
                )
            value = taken.get(c - geo.reach, zero)
            for d in reversed(range(geo.reach)):
                value = jnp.where(picks[d], taken.get(c - d, zero), value)
            taken.pop(c - geo.reach, None)
            index = (word + 8 * c) & (LANES - 1)
            lowest = max((c - geo.reach) * LANES, 0)
            highest = min(c * LANES + LANES - 1, geo.width - 1)
            first_word, last_word = lowest // per_word, highest // per_word
            bits = lane_take(words[first_word], index)
            for w in range(first_word + 1, last_word + 1):
                later = u >= w * per_word - c * LANES
                bits = jnp.where(later, lane_take(words[w], index), bits)
            bits = lax.shift_right_logical(bits, bit) & 1
            if c < geo.reach:
                bits = jnp.where(u >= -c * LANES, bits, 0)
            if c >= flux_chunks:
                bits = jnp.where(u < geo.width - c * LANES, bits, 0)
            good = bits.astype(jnp.float32)
            value = value * good
            high, low = split(value)
            cols = columns(delta + c)
            pf[pl.ds(base, BS), cols] = value
            pm[pl.ds(base, BS), cols] = good
            phl[pl.ds(base, BS), cols] = high
            phl[pl.ds(geo.rows + base, BS), cols] = low
        return carry

    lax.fori_loop(0, NB, body, 0)


def split_table(rank, table, est, cols):
    high, low = split(table[:, cols])
    est[pl.ds(0, rank), cols] = high
    est[pl.ds(rank, rank), cols] = low
    est[pl.ds(2 * rank, rank), cols] = high


def solve(geo, me, pf, pm, phl, est, grad, after=None):
    rank, rows = geo.rank, geo.rows
    start = geo.device_chunk(me)
    step = TILE // LANES
    tiles = geo.win // step
    both = lax.dot_general(
        phl[...],
        est[pl.ds(0, 2 * rank), columns(start, geo.win)],
        (((1,), (1,)), ((), ())),
        preferred_element_type=jnp.float32,
    )
    both = both[:rows] + both[rows:]
    coef = (both[:, :rank] + both[:, rank:]) * geo.scale
    high, low = split(coef * geo.scale)
    high, low = high.astype(jnp.float32), low.astype(jnp.float32)
    left = jnp.concatenate([high, high, low], axis=1).astype(jnp.bfloat16)
    padded = jnp.concatenate([coef, jnp.zeros((rows, LANES - rank), jnp.float32)], axis=1)
    high, low = split(padded.T[:rank])
    high, low = high.astype(jnp.float32), low.astype(jnp.float32)
    across = jnp.concatenate([high, high, low], axis=1).astype(jnp.bfloat16)
    for t in range(tiles):
        cols = pl.ds(t * TILE, TILE)
        band = est[:, columns(start + t * step, step)]
        fit = jnp.dot(left, band, preferred_element_type=jnp.float32)
        resid = pf[:, cols] - pm[:, cols] * fit
        weighted = resid / (1.0 + resid * resid)
        high, low = split(weighted)
        stack = jnp.concatenate([high, low, high], axis=0)
        grad[:, columns(start + t * step, step)] = jnp.dot(
            across, stack, preferred_element_type=jnp.float32
        )
        if after is not None and (t + 1 == tiles or t % 5 == 4):
            after(start + (t + 1) * step, t + 1 == tiles)
    return coef


def plain_kernel(geo, flux_ref, off_ref, word_ref, table_ref, coef_ref, grad_ref, pf, pm, phl, est):
    me = lax.axis_index("gz")
    grad_ref[...] = jnp.zeros_like(grad_ref)
    place(geo, me, flux_ref, off_ref, word_ref, pf, pm, phl)
    start = geo.device_chunk(me)
    for t in range(geo.win * LANES // TILE):
        cols = columns(start + t * (TILE // LANES), TILE // LANES)
        split_table(geo.rank, table_ref, est, cols)
    coef_ref[...] = solve(geo, me, pf, pm, phl, est, grad_ref)


def window_scratch(geo):
    return [
        pltpu.VMEM((geo.rows, geo.window), jnp.float32),
        pltpu.VMEM((geo.rows, geo.window), jnp.float32),
        pltpu.VMEM((2 * geo.rows, geo.window), jnp.bfloat16),
        pltpu.VMEM((3 * geo.rank, geo.pixels), jnp.bfloat16),
    ]


def plain(geo, spectra, offsets, mask_bits, eigen, plan):
    me = lax.axis_index("gz")
    table = lax.all_gather(eigen, "gz", axis=1, tiled=True)
    vmem = pl.BlockSpec(memory_space=pltpu.VMEM)
    smem = pl.BlockSpec(memory_space=pltpu.SMEM)
    coef, grad = pl.pallas_call(
        functools.partial(plain_kernel, geo),
        out_shape=(
            jax.ShapeDtypeStruct((geo.rows, geo.rank), jnp.float32),
            jax.ShapeDtypeStruct((geo.rank, geo.pixels), jnp.float32),
        ),
        in_specs=[vmem, smem, vmem, vmem],
        out_specs=(vmem, vmem),
        scratch_shapes=window_scratch(geo),
        compiler_params=pltpu.CompilerParams(vmem_limit_bytes=40 << 20),
    )(spectra, offsets, mask_bits, table)
    half = plan.shape[0]
    row = lax.dynamic_index_in_dim(plan, me % half, 0, keepdims=False)
    source, block = row[0] == me, row[2]
    blocks = coef.reshape(NB, BS * geo.rank)
    sent = lax.dynamic_index_in_dim(blocks, block, 0, keepdims=True)
    pairs = [(i, (i + half) % geo.devices) for i in range(geo.devices)]
    got = lax.ppermute(sent, "gz", pairs)
    own = jnp.arange(NB, dtype=jnp.int32)[:, None] == block
    blocks = jnp.where(source & own, 0.0, blocks)
    got = jnp.where(source, 0.0, got)
    coefficients = jnp.concatenate([blocks, got], axis=0)[None]
    mine = lax.psum_scatter(grad, "gz", scatter_dimension=1, tiled=True)
    update = eigen + geo.eta * mine
    squares = lax.psum(jnp.sum(update * update, axis=1), "gz")
    eigen_new = update / jnp.sqrt(squares[:, None] / geo.pixels + 1e-06)
    return coefficients, eigen_new


def fused_kernel(
    geo, half, flux_hbm, off_ref, word_hbm, eigen_hbm, plan_ref, coef_ref, new_ref,
    pf, pm, phl, est, flux_ref, word_ref, table, grad, incoming,
    row_out, row_in, coef_out, coef_in, local_done,
    table_sent, table_got, grad_sent, grad_got, row_sent, row_got, coef_sent, coef_got,
):
    me = lax.axis_index("gz")
    devices, rank, rows = geo.devices, geo.rank, geo.rows
    shard = geo.pixels // devices
    per = shard // LANES
    low, high, first, last = geo.ranges(me)

    def peers(body):
        def step(k, carry):
            body(lax.rem(me + k, devices))
            return carry

        lax.fori_loop(1, devices, step, 0)

    def others(start, stop, body):
        def step(k, carry):
            @pl.when(k != me)
            def _():
                body(k)

            return carry

        lax.fori_loop(start, stop, step, 0)

    def table_copy(peer, owner):
        return pltpu.make_async_remote_copy(
            src_ref=eigen_hbm,
            dst_ref=table.at[:, columns(owner * per, per)],
            send_sem=table_sent.at[peer],
            recv_sem=table_got.at[owner],
            device_id={"gz": peer},
            device_id_type=pl.DeviceIdType.MESH,
        )

    def grad_copy(owner, source):
        return pltpu.make_async_remote_copy(
            src_ref=grad.at[:, columns(owner * per, per)],
            dst_ref=incoming.at[source],
            send_sem=grad_sent.at[owner],
            recv_sem=grad_got.at[source],
            device_id={"gz": owner},
            device_id_type=pl.DeviceIdType.MESH,
        )

    def row_copy(peer, source):
        return pltpu.make_async_remote_copy(
            src_ref=row_out,
            dst_ref=row_in.at[source],
            send_sem=row_sent.at[peer],
            recv_sem=row_got.at[source],
            device_id={"gz": peer},
            device_id_type=pl.DeviceIdType.MESH,
        )

    copies = [
        pltpu.make_async_copy(flux_hbm, flux_ref, local_done.at[0]),
        pltpu.make_async_copy(word_hbm, word_ref, local_done.at[1]),
        pltpu.make_async_copy(eigen_hbm, table.at[:, columns(me * per, per)], local_done.at[2]),
    ]
    for copy in copies:
        copy.start()
    barrier = pltpu.get_barrier_semaphore()
    peers(lambda peer: pl.semaphore_signal(
        barrier, inc=1, device_id={"gz": peer}, device_id_type=pl.DeviceIdType.MESH
    ))
    pl.semaphore_wait(barrier, devices - 1)
    def send(i, carry):
        half_way = lax.div(i, 2)
        peer = jnp.where(lax.rem(i, 2) == 0, first + half_way, last - half_way)

        @pl.when(peer != me)
        def _():
            table_copy(peer, me).start()

        return carry

    lax.fori_loop(0, last - first + 1, send, 0)
    grad[...] = jnp.zeros_like(grad)
    copies[0].wait()
    copies[1].wait()
    place(geo, me, flux_ref, off_ref, word_ref, pf, pm, phl)
    copies[2].wait()

    def receive(i, carry):
        turn = me + i
        owner = jnp.where(turn > high, turn - (high + 1 - low), turn)

        @pl.when(owner != me)
        def _():
            table_copy(owner, owner).wait_recv()

        split_table(rank, table, est, columns(owner * per, per))
        return carry

    lax.fori_loop(0, high + 1 - low, receive, 0)
    begun = [low]

    def after(chunk, done):
        stop = high + 1 if done else lax.div(chunk, per)
        others(begun[0], stop, lambda owner: grad_copy(owner, me).start())
        begun[0] = stop

    coef = solve(geo, me, pf, pm, phl, est, grad, after)

    padded = jnp.concatenate([coef, jnp.zeros((rows, LANES - rank), jnp.float32)], axis=1)
    lane = lax.broadcasted_iota(jnp.int32, (BS, LANES), 1)
    row = lax.broadcasted_iota(jnp.int32, (BS, LANES), 0)
    plan_row = lax.rem(me, half)
    source, block = plan_ref[0, plan_row], plan_ref[2, plan_row]
    group = LANES // rank
    for h in range(BS // group):
        here = row == lax.div(lane, rank) + h * group
        cols = pl.ds(h * LANES, LANES)
        sent = jnp.zeros((1, LANES), jnp.float32)
        for b in range(NB):
            spread = lane_take(padded[b * BS:(b + 1) * BS], lane & (rank - 1))
            flat = jnp.sum(jnp.where(here, spread, 0.0), axis=0, keepdims=True)
            planned = jnp.where(block == b, 1.0, 0.0)
            gone = planned * jnp.where(source == me, 1.0, 0.0)
            sent = sent + flat * planned
            coef_ref[0, pl.ds(b, 1), cols] = flat * (1.0 - gone)
        coef_out[:, cols] = sent
    partner = lax.rem(me + half, devices)
    coef_copy = pltpu.make_async_remote_copy(
        src_ref=coef_out,
        dst_ref=coef_in,
        send_sem=coef_sent,
        recv_sem=coef_got,
        device_id={"gz": partner},
        device_id_type=pl.DeviceIdType.MESH,
    )
    coef_copy.start()

    new_ref[...] = grad[:, columns(me * per, per)]

    def add(peer):
        grad_copy(me, peer).wait_recv()
        new_ref[...] += incoming[peer]

    others(first, last + 1, add)
    update = table[:, columns(me * per, per)] + geo.eta * new_ref[...]
    new_ref[...] = update
    squares = jnp.sum(update * update, axis=1, keepdims=True)
    wide = lax.broadcasted_iota(jnp.int32, (rank, LANES), 1)
    tall = lax.broadcasted_iota(jnp.int32, (rank, LANES), 0)
    diagonal = wide == tall
    packed = jnp.sum(jnp.where(diagonal, squares, 0.0), axis=0, keepdims=True)
    row_out[...] = packed
    peers(lambda peer: row_copy(peer, me).start())
    coef_copy.wait()
    coef_ref[0, pl.ds(NB, 1), :] = coef_in[...] * jnp.where(source == me, 0.0, 1.0)
    row_in[me] = packed
    peers(lambda peer: row_copy(peer, peer).wait_recv())
    total = row_in[0]
    for d in range(1, devices):
        total = total + row_in[d]
    mean = jnp.sum(jnp.where(diagonal, total, 0.0), axis=1, keepdims=True) / geo.pixels
    new_ref[...] = new_ref[...] / jnp.sqrt(mean + 1e-06)

    peers(lambda peer: row_copy(peer, me).wait_send())
    others(first, last + 1, lambda peer: table_copy(peer, me).wait_send())
    others(low, high + 1, lambda owner: grad_copy(owner, me).wait_send())


def fused(geo, spectra, offsets, mask_bits, eigen, plan):
    vmem = pl.BlockSpec(memory_space=pltpu.VMEM)
    smem = pl.BlockSpec(memory_space=pltpu.SMEM)
    hbm = pl.BlockSpec(memory_space=pltpu.HBM)
    shard = geo.pixels // geo.devices
    width = BS * geo.rank
    many = pltpu.SemaphoreType.DMA((geo.devices,))
    one = pltpu.SemaphoreType.DMA
    return pl.pallas_call(
        functools.partial(fused_kernel, geo, plan.shape[0]),
        out_shape=(
            jax.ShapeDtypeStruct((1, NB + 1, width), jnp.float32),
            jax.ShapeDtypeStruct((geo.rank, shard), jnp.float32),
        ),
        in_specs=[hbm, smem, hbm, hbm, smem],
        out_specs=(vmem, vmem),
        scratch_shapes=window_scratch(geo) + [
            pltpu.VMEM(spectra.shape, jnp.float32),
            pltpu.VMEM(mask_bits.shape, jnp.int32),
            pltpu.VMEM((geo.rank, geo.pixels), jnp.float32),
            pltpu.VMEM((geo.rank, geo.pixels), jnp.float32),
            pltpu.VMEM((geo.devices, geo.rank, shard), jnp.float32),
            pltpu.VMEM((1, LANES), jnp.float32),
            pltpu.VMEM((geo.devices, 1, LANES), jnp.float32),
            pltpu.VMEM((1, width), jnp.float32),
            pltpu.VMEM((1, width), jnp.float32),
            pltpu.SemaphoreType.DMA((3,)),
            many, many, many, many, many, many, one, one,
        ],
        compiler_params=pltpu.CompilerParams(
            vmem_limit_bytes=64 << 20, collective_id=0, has_side_effects=True
        ),
    )(spectra, offsets, mask_bits, eigen, plan.T)


def local(spectra, offsets, mask_bits, eigen, plan):
    devices = lax.axis_size("gz")
    rank, shard = eigen.shape
    geo = Geometry(devices, spectra.shape[0], spectra.shape[1], shard * devices, rank)
    if shard % LANES == 0:
        return fused(geo, spectra, offsets, mask_bits, eigen, plan)
    return plain(geo, spectra, offsets, mask_bits, eigen, plan)


def solution(mesh):
    placed = (
        P(("grp", "gz"), None),
        P(("grp", "gz")),
        P(("grp", "gz"), None),
        P(None, "gz"),
        P("grp", None),
    )
    return jax.shard_map(
        local,
        mesh=mesh,
        in_specs=placed,
        out_specs=(P(("grp", "gz"), None, None), P("grp", "gz")),
        check_vma=False,
    )
```

```python
import functools
import math

import jax
import jax.numpy as jnp
from jax import lax
from jax.experimental import pallas as pl
from jax.experimental.pallas import tpu as pltpu
from jax.sharding import PartitionSpec as P

NB = 4
BS = 16
SPAN = 128
LANES = 128
TILE = 256
GROUP = 4


class Geometry:
    def __init__(self, devices, rows, width, pixels, rank):
        self.devices, self.rows, self.width = devices, rows, width
        self.pixels, self.rank = pixels, rank
        self.total = devices * rows
        self.ramp = pixels - width - SPAN
        per_block = ((BS - 1) * self.ramp) // self.total + 1
        self.reach = -(-(per_block + SPAN + LANES - 1) // LANES)
        self.sub = width // LANES + self.reach
        lead = (((NB - 1) * BS * self.ramp) // self.total + LANES) // LANES
        win = self.sub + lead
        self.win = win + win % 2
        self.window = self.win * LANES
        self.scale = 1.0 / math.sqrt(width)
        self.eta = 2.0 / math.sqrt(self.total * width / pixels)

    def aligned(self, spectrum, chunks):
        start = lax.div(lax.div(spectrum * self.ramp, self.total), LANES)
        return jnp.minimum(start, self.pixels // LANES - chunks)

    def static_range(self, device):
        first = min(device * self.rows * self.ramp // self.total // LANES,
                    self.pixels // LANES - self.win)
        per = self.pixels // self.devices // LANES
        return first // per, (first + self.win - 1) // per

    def ranges(self, me):
        shards = [self.static_range(d) for d in range(self.devices)]
        low, high, first, last = 0, 0, 0, -1
        for d, (a, b) in enumerate(shards):
            low = jnp.where(me == d, a, low)
            high = jnp.where(me == d, b, high)
            first = first + jnp.where(me > b, 1, 0)
            last = last + jnp.where(me >= a, 1, 0)
        return low, high, first, last

    def device_chunk(self, device):
        return self.aligned(device * self.rows, self.win)

    def block_chunk(self, device, block):
        return self.aligned(device * self.rows + block * BS, self.sub)


def split(x):
    high = x.astype(jnp.bfloat16)
    low = (x - high.astype(jnp.float32)).astype(jnp.bfloat16)
    return high, low


def columns(chunk, count=1):
    return pl.ds(pl.multiple_of(chunk * LANES, LANES), count * LANES)


def lane_take(x, index):
    return jnp.take_along_axis(x, index, axis=1, mode="promise_in_bounds")


def place(geo, me, flux_ref, off_ref, word_ref, pf, pm, phl):
    edge = max(geo.win - geo.sub, 1)
    for lo in (0, geo.win - edge):
        cols = pl.ds(lo * LANES, edge * LANES)
        pf[:, cols] = jnp.zeros((geo.rows, edge * LANES), jnp.float32)
        pm[:, cols] = jnp.zeros((geo.rows, edge * LANES), jnp.float32)
        phl[:, cols] = jnp.zeros((2 * geo.rows, edge * LANES), jnp.bfloat16)
    device_chunk = geo.device_chunk(me)
    lane = lax.broadcasted_iota(jnp.int32, (BS, LANES), 1)
    row = lax.broadcasted_iota(jnp.int32, (BS, LANES), 0)
    flux_chunks = geo.width // LANES

    def body(block, carry):
        first = geo.block_chunk(me, block)
        delta = first - device_chunk
        base = pl.multiple_of(block * BS, BS)
        offs = jnp.zeros((BS, LANES), jnp.int32)
        for s in range(BS):
            offs = jnp.where(row == s, off_ref[base + s], offs)
        u = lane - (offs - first * LANES)
        back = lax.shift_right_arithmetic(u, 7)
        lane_index = u & (LANES - 1)
        bit = u & 15
        word = lax.shift_right_arithmetic(u, 4)
        picks = [back == -d for d in range(geo.reach)]
        zero = jnp.zeros((BS, LANES), jnp.float32)
        words = [
            word_ref[pl.ds(base, BS), pl.ds(i * LANES, LANES)]
            for i in range(geo.width // 16 // LANES)
        ]
        per_word = 16 * LANES
        taken = {}
        for c in range(geo.sub):
            if c < flux_chunks:
                taken[c] = lane_take(
                    flux_ref[pl.ds(base, BS), pl.ds(c * LANES, LANES)], lane_index
                )
            value = taken.get(c - geo.reach, zero)
            for d in reversed(range(geo.reach)):
                value = jnp.where(picks[d], taken.get(c - d, zero), value)
            taken.pop(c - geo.reach, None)
            index = (word + 8 * c) & (LANES - 1)
            lowest = max((c - geo.reach) * LANES, 0)
            highest = min(c * LANES + LANES - 1, geo.width - 1)
            first_word, last_word = lowest // per_word, highest // per_word
            bits = lane_take(words[first_word], index)
            for w in range(first_word + 1, last_word + 1):
                later = u >= w * per_word - c * LANES
                bits = jnp.where(later, lane_take(words[w], index), bits)
            bits = lax.shift_right_logical(bits, bit) & 1
            if c < geo.reach:
                bits = jnp.where(u >= -c * LANES, bits, 0)
            if c >= flux_chunks:
                bits = jnp.where(u < geo.width - c * LANES, bits, 0)
            good = bits.astype(jnp.float32)
            value = value * good
            high, low = split(value)
            cols = columns(delta + c)
            pf[pl.ds(base, BS), cols] = value
            pm[pl.ds(base, BS), cols] = good
            phl[pl.ds(base, BS), cols] = high
            phl[pl.ds(geo.rows + base, BS), cols] = low
        return carry

    lax.fori_loop(0, NB, body, 0)


def split_table(rank, table, est, cols):
    high, low = split(table[:, cols])
    est[pl.ds(0, rank), cols] = high
    est[pl.ds(rank, rank), cols] = low
    est[pl.ds(2 * rank, rank), cols] = high


def solve(geo, me, pf, pm, phl, est, grad, after=None):
    rank, rows = geo.rank, geo.rows
    start = geo.device_chunk(me)
    step = TILE // LANES
    tiles = geo.win // step
    both = lax.dot_general(
        phl[...],
        est[pl.ds(0, 2 * rank), columns(start, geo.win)],
        (((1,), (1,)), ((), ())),
        preferred_element_type=jnp.float32,
    )
    both = both[:rows] + both[rows:]
    coef = (both[:, :rank] + both[:, rank:]) * geo.scale
    high, low = split(coef * geo.scale)
    high, low = high.astype(jnp.float32), low.astype(jnp.float32)
    left = jnp.concatenate([high, high, low], axis=1).astype(jnp.bfloat16)
    padded = jnp.concatenate([coef, jnp.zeros((rows, LANES - rank), jnp.float32)], axis=1)
    high, low = split(padded.T[:rank])
    high, low = high.astype(jnp.float32), low.astype(jnp.float32)
    across = jnp.concatenate([high, high, low], axis=1).astype(jnp.bfloat16)
    for t in range(tiles):
        cols = pl.ds(t * TILE, TILE)
        band = est[:, columns(start + t * step, step)]
        fit = jnp.dot(left, band, preferred_element_type=jnp.float32)
        resid = pf[:, cols] - pm[:, cols] * fit
        weighted = resid / (1.0 + resid * resid)
        high, low = split(weighted)
        stack = jnp.concatenate([high, low, high], axis=0)
        grad[:, columns(start + t * step, step)] = jnp.dot(
            across, stack, preferred_element_type=jnp.float32
        )
        if after is not None and (t + 1 == tiles or t % 5 == 4):
            after(start + (t + 1) * step, t + 1 == tiles)
    return coef


def plain_kernel(geo, flux_ref, off_ref, word_ref, table_ref, coef_ref, grad_ref, pf, pm, phl, est):
    me = lax.axis_index("gz")
    grad_ref[...] = jnp.zeros_like(grad_ref)
    place(geo, me, flux_ref, off_ref, word_ref, pf, pm, phl)
    start = geo.device_chunk(me)
    for t in range(geo.win * LANES // TILE):
        cols = columns(start + t * (TILE // LANES), TILE // LANES)
        split_table(geo.rank, table_ref, est, cols)
    coef_ref[...] = solve(geo, me, pf, pm, phl, est, grad_ref)


def window_scratch(geo):
    return [
        pltpu.VMEM((geo.rows, geo.window), jnp.float32),
        pltpu.VMEM((geo.rows, geo.window), jnp.float32),
        pltpu.VMEM((2 * geo.rows, geo.window), jnp.bfloat16),
        pltpu.VMEM((3 * geo.rank, geo.pixels), jnp.bfloat16),
    ]


def plain(geo, spectra, offsets, mask_bits, eigen, plan):
    me = lax.axis_index("gz")
    table = lax.all_gather(eigen, "gz", axis=1, tiled=True)
    vmem = pl.BlockSpec(memory_space=pltpu.VMEM)
    smem = pl.BlockSpec(memory_space=pltpu.SMEM)
    coef, grad = pl.pallas_call(
        functools.partial(plain_kernel, geo),
        out_shape=(
            jax.ShapeDtypeStruct((geo.rows, geo.rank), jnp.float32),
            jax.ShapeDtypeStruct((geo.rank, geo.pixels), jnp.float32),
        ),
        in_specs=[vmem, smem, vmem, vmem],
        out_specs=(vmem, vmem),
        scratch_shapes=window_scratch(geo),
        compiler_params=pltpu.CompilerParams(vmem_limit_bytes=40 << 20),
    )(spectra, offsets, mask_bits, table)
    half = plan.shape[0]
    row = lax.dynamic_index_in_dim(plan, me % half, 0, keepdims=False)
    source, block = row[0] == me, row[2]
    blocks = coef.reshape(NB, BS * geo.rank)
    sent = lax.dynamic_index_in_dim(blocks, block, 0, keepdims=True)
    pairs = [(i, (i + half) % geo.devices) for i in range(geo.devices)]
    got = lax.ppermute(sent, "gz", pairs)
    own = jnp.arange(NB, dtype=jnp.int32)[:, None] == block
    blocks = jnp.where(source & own, 0.0, blocks)
    got = jnp.where(source, 0.0, got)
    coefficients = jnp.concatenate([blocks, got], axis=0)[None]
    mine = lax.psum_scatter(grad, "gz", scatter_dimension=1, tiled=True)
    update = eigen + geo.eta * mine
    squares = lax.psum(jnp.sum(update * update, axis=1), "gz")
    eigen_new = update / jnp.sqrt(squares[:, None] / geo.pixels + 1e-06)
    return coefficients, eigen_new


def fused_kernel(
    geo, half, flux_hbm, off_ref, word_hbm, eigen_hbm, plan_ref, coef_ref, new_ref,
    pf, pm, phl, est, flux_ref, word_ref, table, grad, incoming,
    row_out, row_mid, row_in, coef_out, coef_in, local_done,
    table_sent, table_got, grad_sent, grad_got, row_sent, row_got, coef_sent, coef_got,
):
    me = lax.axis_index("gz")
    devices, rank, rows = geo.devices, geo.rank, geo.rows
    shard = geo.pixels // devices
    per = shard // LANES
    low, high, first, last = geo.ranges(me)

    def peers(body):
        def step(k, carry):
            body(lax.rem(me + k, devices))
            return carry

        lax.fori_loop(1, devices, step, 0)

    def others(start, stop, body):
        def step(k, carry):
            @pl.when(k != me)
            def _():
                body(k)

            return carry

        lax.fori_loop(start, stop, step, 0)

    def table_copy(peer, owner):
        return pltpu.make_async_remote_copy(
            src_ref=eigen_hbm,
            dst_ref=table.at[:, columns(owner * per, per)],
            send_sem=table_sent.at[peer],
            recv_sem=table_got.at[owner],
            device_id={"gz": peer},
            device_id_type=pl.DeviceIdType.MESH,
        )

    def grad_copy(owner, source):
        return pltpu.make_async_remote_copy(
            src_ref=grad.at[:, columns(owner * per, per)],
            dst_ref=incoming.at[source],
            send_sem=grad_sent.at[owner],
            recv_sem=grad_got.at[source],
            device_id={"gz": owner},
            device_id_type=pl.DeviceIdType.MESH,
        )

    def row_copy(peer, source, row_from):
        return pltpu.make_async_remote_copy(
            src_ref=row_from,
            dst_ref=row_in.at[source],
            send_sem=row_sent.at[peer],
            recv_sem=row_got.at[source],
            device_id={"gz": peer},
            device_id_type=pl.DeviceIdType.MESH,
        )

    copies = [
        pltpu.make_async_copy(flux_hbm, flux_ref, local_done.at[0]),
        pltpu.make_async_copy(word_hbm, word_ref, local_done.at[1]),
        pltpu.make_async_copy(eigen_hbm, table.at[:, columns(me * per, per)], local_done.at[2]),
    ]
    for copy in copies:
        copy.start()
    barrier = pltpu.get_barrier_semaphore()
    peers(lambda peer: pl.semaphore_signal(
        barrier, inc=1, device_id={"gz": peer}, device_id_type=pl.DeviceIdType.MESH
    ))
    pl.semaphore_wait(barrier, devices - 1)
    def send(i, carry):
        half_way = lax.div(i, 2)
        peer = jnp.where(lax.rem(i, 2) == 0, first + half_way, last - half_way)

        @pl.when(peer != me)
        def _():
            table_copy(peer, me).start()

        return carry

    lax.fori_loop(0, last - first + 1, send, 0)
    grad[...] = jnp.zeros_like(grad)
    copies[0].wait()
    copies[1].wait()
    place(geo, me, flux_ref, off_ref, word_ref, pf, pm, phl)
    copies[2].wait()

    def receive(i, carry):
        turn = me + i
        owner = jnp.where(turn > high, turn - (high + 1 - low), turn)

        @pl.when(owner != me)
        def _():
            table_copy(owner, owner).wait_recv()

        split_table(rank, table, est, columns(owner * per, per))
        return carry

    lax.fori_loop(0, high + 1 - low, receive, 0)
    begun = [low]

    def after(chunk, done):
        stop = high + 1 if done else lax.div(chunk, per)
        others(begun[0], stop, lambda owner: grad_copy(owner, me).start())
        begun[0] = stop

    coef = solve(geo, me, pf, pm, phl, est, grad, after)

    padded = jnp.concatenate([coef, jnp.zeros((rows, LANES - rank), jnp.float32)], axis=1)
    lane = lax.broadcasted_iota(jnp.int32, (BS, LANES), 1)
    row = lax.broadcasted_iota(jnp.int32, (BS, LANES), 0)
    plan_row = lax.rem(me, half)
    source, block = plan_ref[0, plan_row], plan_ref[2, plan_row]
    group = LANES // rank
    for h in range(BS // group):
        here = row == lax.div(lane, rank) + h * group
        cols = pl.ds(h * LANES, LANES)
        sent = jnp.zeros((1, LANES), jnp.float32)
        for b in range(NB):
            spread = lane_take(padded[b * BS:(b + 1) * BS], lane & (rank - 1))
            flat = jnp.sum(jnp.where(here, spread, 0.0), axis=0, keepdims=True)
            planned = jnp.where(block == b, 1.0, 0.0)
            gone = planned * jnp.where(source == me, 1.0, 0.0)
            sent = sent + flat * planned
            coef_ref[0, pl.ds(b, 1), cols] = flat * (1.0 - gone)
        coef_out[:, cols] = sent
    partner = lax.rem(me + half, devices)
    coef_copy = pltpu.make_async_remote_copy(
        src_ref=coef_out,
        dst_ref=coef_in,
        send_sem=coef_sent,
        recv_sem=coef_got,
        device_id={"gz": partner},
        device_id_type=pl.DeviceIdType.MESH,
    )
    coef_copy.start()

    new_ref[...] = grad[:, columns(me * per, per)]

    def add(peer):
        grad_copy(me, peer).wait_recv()
        new_ref[...] += incoming[peer]

    others(first, last + 1, add)
    update = table[:, columns(me * per, per)] + geo.eta * new_ref[...]
    new_ref[...] = update
    squares = jnp.sum(update * update, axis=1, keepdims=True)
    wide = lax.broadcasted_iota(jnp.int32, (rank, LANES), 1)
    tall = lax.broadcasted_iota(jnp.int32, (rank, LANES), 0)
    diagonal = wide == tall
    packed = jnp.sum(jnp.where(diagonal, squares, 0.0), axis=0, keepdims=True)
    row_out[...] = packed
    team = GROUP if devices % GROUP == 0 else devices
    base = lax.div(me, team) * team
    place_in = lax.rem(me, team)
    near = [base + lax.rem(place_in + k, team) for k in range(1, team)]
    far = [lax.rem(me + k * team, devices) for k in range(1, devices // team)]
    row_in[me] = packed
    for peer in near:
        row_copy(peer, me, row_out).start()
    coef_copy.wait()
    coef_ref[0, pl.ds(NB, 1), :] = coef_in[...] * jnp.where(source == me, 0.0, 1.0)
    for peer in near:
        row_copy(peer, peer, row_out).wait_recv()
    total = row_in[base]
    for d in range(1, team):
        total = total + row_in[base + d]
    row_mid[...] = total
    for peer in far:
        row_copy(peer, me, row_mid).start()
    row_in[me] = total
    for peer in far:
        row_copy(peer, peer, row_mid).wait_recv()
    total = row_in[place_in]
    for d in range(1, devices // team):
        total = total + row_in[place_in + d * team]
    mean = jnp.sum(jnp.where(diagonal, total, 0.0), axis=1, keepdims=True) / geo.pixels
    new_ref[...] = new_ref[...] / jnp.sqrt(mean + 1e-06)

    for peer in near:
        row_copy(peer, me, row_out).wait_send()
    for peer in far:
        row_copy(peer, me, row_mid).wait_send()
    others(first, last + 1, lambda peer: table_copy(peer, me).wait_send())
    others(low, high + 1, lambda owner: grad_copy(owner, me).wait_send())


def fused(geo, spectra, offsets, mask_bits, eigen, plan):
    vmem = pl.BlockSpec(memory_space=pltpu.VMEM)
    smem = pl.BlockSpec(memory_space=pltpu.SMEM)
    hbm = pl.BlockSpec(memory_space=pltpu.HBM)
    shard = geo.pixels // geo.devices
    width = BS * geo.rank
    many = pltpu.SemaphoreType.DMA((geo.devices,))
    one = pltpu.SemaphoreType.DMA
    return pl.pallas_call(
        functools.partial(fused_kernel, geo, plan.shape[0]),
        out_shape=(
            jax.ShapeDtypeStruct((1, NB + 1, width), jnp.float32),
            jax.ShapeDtypeStruct((geo.rank, shard), jnp.float32),
        ),
        in_specs=[hbm, smem, hbm, hbm, smem],
        out_specs=(vmem, vmem),
        scratch_shapes=window_scratch(geo) + [
            pltpu.VMEM(spectra.shape, jnp.float32),
            pltpu.VMEM(mask_bits.shape, jnp.int32),
            pltpu.VMEM((geo.rank, geo.pixels), jnp.float32),
            pltpu.VMEM((geo.rank, geo.pixels), jnp.float32),
            pltpu.VMEM((geo.devices, geo.rank, shard), jnp.float32),
            pltpu.VMEM((1, LANES), jnp.float32),
            pltpu.VMEM((1, LANES), jnp.float32),
            pltpu.VMEM((geo.devices, 1, LANES), jnp.float32),
            pltpu.VMEM((1, width), jnp.float32),
            pltpu.VMEM((1, width), jnp.float32),
            pltpu.SemaphoreType.DMA((3,)),
            many, many, many, many, many, many, one, one,
        ],
        compiler_params=pltpu.CompilerParams(
            vmem_limit_bytes=64 << 20, collective_id=0, has_side_effects=True
        ),
    )(spectra, offsets, mask_bits, eigen, plan.T)


def local(spectra, offsets, mask_bits, eigen, plan):
    devices = lax.axis_size("gz")
    rank, shard = eigen.shape
    geo = Geometry(devices, spectra.shape[0], spectra.shape[1], shard * devices, rank)
    if shard % LANES == 0:
        return fused(geo, spectra, offsets, mask_bits, eigen, plan)
    return plain(geo, spectra, offsets, mask_bits, eigen, plan)


def solution(mesh):
    placed = (
        P(("grp", "gz"), None),
        P(("grp", "gz")),
        P(("grp", "gz"), None),
        P(None, "gz"),
        P("grp", None),
    )
    return jax.shard_map(
        local,
        mesh=mesh,
        in_specs=placed,
        out_specs=(P(("grp", "gz"), None, None), P("grp", "gz")),
        check_vma=False,
    )
```

```python
import functools
import math

import jax
import jax.numpy as jnp
from jax import lax
from jax.experimental import pallas as pl
from jax.experimental.pallas import tpu as pltpu
from jax.sharding import PartitionSpec as P

NB = 4
BS = 16
SPAN = 128
LANES = 128
TILE = 256


class Geometry:
    def __init__(self, devices, rows, width, pixels, rank):
        self.devices, self.rows, self.width = devices, rows, width
        self.pixels, self.rank = pixels, rank
        self.total = devices * rows
        self.ramp = pixels - width - SPAN
        per_block = ((BS - 1) * self.ramp) // self.total + 1
        self.reach = -(-(per_block + SPAN + LANES - 1) // LANES)
        self.sub = width // LANES + self.reach
        lead = (((NB - 1) * BS * self.ramp) // self.total + LANES) // LANES
        win = self.sub + lead
        self.win = win + win % 2
        self.window = self.win * LANES
        self.scale = 1.0 / math.sqrt(width)
        self.eta = 2.0 / math.sqrt(self.total * width / pixels)

    def aligned(self, spectrum, chunks):
        start = lax.div(lax.div(spectrum * self.ramp, self.total), LANES)
        return jnp.minimum(start, self.pixels // LANES - chunks)

    def static_range(self, device):
        first = min(device * self.rows * self.ramp // self.total // LANES,
                    self.pixels // LANES - self.win)
        per = self.pixels // self.devices // LANES
        return first // per, (first + self.win - 1) // per

    def ranges(self, me):
        shards = [self.static_range(d) for d in range(self.devices)]
        low, high, first, last = 0, 0, 0, -1
        for d, (a, b) in enumerate(shards):
            low = jnp.where(me == d, a, low)
            high = jnp.where(me == d, b, high)
            first = first + jnp.where(me > b, 1, 0)
            last = last + jnp.where(me >= a, 1, 0)
        return low, high, first, last

    def device_chunk(self, device):
        return self.aligned(device * self.rows, self.win)

    def block_chunk(self, device, block):
        return self.aligned(device * self.rows + block * BS, self.sub)


def split(x):
    high = x.astype(jnp.bfloat16)
    low = (x - high.astype(jnp.float32)).astype(jnp.bfloat16)
    return high, low


def columns(chunk, count=1):
    return pl.ds(pl.multiple_of(chunk * LANES, LANES), count * LANES)


def lane_take(x, index):
    return jnp.take_along_axis(x, index, axis=1, mode="promise_in_bounds")


def place(geo, me, flux_ref, off_ref, word_ref, pf, pm, phl):
    edge = max(geo.win - geo.sub, 1)
    for lo in (0, geo.win - edge):
        cols = pl.ds(lo * LANES, edge * LANES)
        pf[:, cols] = jnp.zeros((geo.rows, edge * LANES), jnp.float32)
        pm[:, cols] = jnp.zeros((geo.rows, edge * LANES), jnp.float32)
        phl[:, cols] = jnp.zeros((2 * geo.rows, edge * LANES), jnp.bfloat16)
    device_chunk = geo.device_chunk(me)
    lane = lax.broadcasted_iota(jnp.int32, (BS, LANES), 1)
    row = lax.broadcasted_iota(jnp.int32, (BS, LANES), 0)
    flux_chunks = geo.width // LANES

    def body(block, carry):
        first = geo.block_chunk(me, block)
        delta = first - device_chunk
        base = pl.multiple_of(block * BS, BS)
        offs = jnp.zeros((BS, LANES), jnp.int32)
        for s in range(BS):
            offs = jnp.where(row == s, off_ref[base + s], offs)
        u = lane - (offs - first * LANES)
        back = lax.shift_right_arithmetic(u, 7)
        lane_index = u & (LANES - 1)
        bit = u & 15
        word = lax.shift_right_arithmetic(u, 4)
        picks = [back == -d for d in range(geo.reach)]
        zero = jnp.zeros((BS, LANES), jnp.float32)
        words = [
            word_ref[pl.ds(base, BS), pl.ds(i * LANES, LANES)]
            for i in range(geo.width // 16 // LANES)
        ]
        per_word = 16 * LANES
        taken = {}
        for c in range(geo.sub):
            if c < flux_chunks:
                taken[c] = lane_take(
                    flux_ref[pl.ds(base, BS), pl.ds(c * LANES, LANES)], lane_index
                )
            value = taken.get(c - geo.reach, zero)
            for d in reversed(range(geo.reach)):
                value = jnp.where(picks[d], taken.get(c - d, zero), value)
            taken.pop(c - geo.reach, None)
            index = (word + 8 * c) & (LANES - 1)
            lowest = max((c - geo.reach) * LANES, 0)
            highest = min(c * LANES + LANES - 1, geo.width - 1)
            first_word, last_word = lowest // per_word, highest // per_word
            bits = lane_take(words[first_word], index)
            for w in range(first_word + 1, last_word + 1):
                later = u >= w * per_word - c * LANES
                bits = jnp.where(later, lane_take(words[w], index), bits)
            bits = lax.shift_right_logical(bits, bit) & 1
            if c < geo.reach:
                bits = jnp.where(u >= -c * LANES, bits, 0)
            if c >= flux_chunks:
                bits = jnp.where(u < geo.width - c * LANES, bits, 0)
            good = bits.astype(jnp.float32)
            value = value * good
            high, low = split(value)
            cols = columns(delta + c)
            pf[pl.ds(base, BS), cols] = value
            pm[pl.ds(base, BS), cols] = good
            phl[pl.ds(base, BS), cols] = high
            phl[pl.ds(geo.rows + base, BS), cols] = low
        return carry

    lax.fori_loop(0, NB, body, 0)


def split_table(rank, table, est, cols):
    high, low = split(table[:, cols])
    est[pl.ds(0, rank), cols] = high
    est[pl.ds(rank, rank), cols] = low
    est[pl.ds(2 * rank, rank), cols] = high


def solve(geo, me, pf, pm, phl, est, grad, after=None):
    rank, rows = geo.rank, geo.rows
    start = geo.device_chunk(me)
    step = TILE // LANES
    tiles = geo.win // step
    both = lax.dot_general(
        phl[...],
        est[pl.ds(0, 2 * rank), columns(start, geo.win)],
        (((1,), (1,)), ((), ())),
        preferred_element_type=jnp.float32,
    )
    both = both[:rows] + both[rows:]
    coef = (both[:, :rank] + both[:, rank:]) * geo.scale
    high, low = split(coef * geo.scale)
    high, low = high.astype(jnp.float32), low.astype(jnp.float32)
    left = jnp.concatenate([high, high, low], axis=1).astype(jnp.bfloat16)
    padded = jnp.concatenate([coef, jnp.zeros((rows, LANES - rank), jnp.float32)], axis=1)
    high, low = split(padded.T[:rank])
    high, low = high.astype(jnp.float32), low.astype(jnp.float32)
    across = jnp.concatenate([high, high, low], axis=1).astype(jnp.bfloat16)
    for t in range(tiles):
        cols = pl.ds(t * TILE, TILE)
        band = est[:, columns(start + t * step, step)]
        fit = jnp.dot(left, band, preferred_element_type=jnp.float32)
        resid = pf[:, cols] - pm[:, cols] * fit
        weighted = resid / (1.0 + resid * resid)
        high, low = split(weighted)
        stack = jnp.concatenate([high, low, high], axis=0)
        grad[:, columns(start + t * step, step)] = jnp.dot(
            across, stack, preferred_element_type=jnp.float32
        )
        if after is not None and (t + 1 == tiles or t % 5 == 4):
            after(start + (t + 1) * step, t + 1 == tiles)
    return coef


def plain_kernel(geo, flux_ref, off_ref, word_ref, table_ref, coef_ref, grad_ref, pf, pm, phl, est):
    me = lax.axis_index("gz")
    grad_ref[...] = jnp.zeros_like(grad_ref)
    place(geo, me, flux_ref, off_ref, word_ref, pf, pm, phl)
    start = geo.device_chunk(me)
    for t in range(geo.win * LANES // TILE):
        cols = columns(start + t * (TILE // LANES), TILE // LANES)
        split_table(geo.rank, table_ref, est, cols)
    coef_ref[...] = solve(geo, me, pf, pm, phl, est, grad_ref)


def window_scratch(geo):
    return [
        pltpu.VMEM((geo.rows, geo.window), jnp.float32),
        pltpu.VMEM((geo.rows, geo.window), jnp.float32),
        pltpu.VMEM((2 * geo.rows, geo.window), jnp.bfloat16),
        pltpu.VMEM((3 * geo.rank, geo.pixels), jnp.bfloat16),
    ]


def plain(geo, spectra, offsets, mask_bits, eigen, plan):
    me = lax.axis_index("gz")
    table = lax.all_gather(eigen, "gz", axis=1, tiled=True)
    vmem = pl.BlockSpec(memory_space=pltpu.VMEM)
    smem = pl.BlockSpec(memory_space=pltpu.SMEM)
    coef, grad = pl.pallas_call(
        functools.partial(plain_kernel, geo),
        out_shape=(
            jax.ShapeDtypeStruct((geo.rows, geo.rank), jnp.float32),
            jax.ShapeDtypeStruct((geo.rank, geo.pixels), jnp.float32),
        ),
        in_specs=[vmem, smem, vmem, vmem],
        out_specs=(vmem, vmem),
        scratch_shapes=window_scratch(geo),
        compiler_params=pltpu.CompilerParams(vmem_limit_bytes=40 << 20),
    )(spectra, offsets, mask_bits, table)
    half = plan.shape[0]
    row = lax.dynamic_index_in_dim(plan, me % half, 0, keepdims=False)
    source, block = row[0] == me, row[2]
    blocks = coef.reshape(NB, BS * geo.rank)
    sent = lax.dynamic_index_in_dim(blocks, block, 0, keepdims=True)
    pairs = [(i, (i + half) % geo.devices) for i in range(geo.devices)]
    got = lax.ppermute(sent, "gz", pairs)
    own = jnp.arange(NB, dtype=jnp.int32)[:, None] == block
    blocks = jnp.where(source & own, 0.0, blocks)
    got = jnp.where(source, 0.0, got)
    coefficients = jnp.concatenate([blocks, got], axis=0)[None]
    mine = lax.psum_scatter(grad, "gz", scatter_dimension=1, tiled=True)
    update = eigen + geo.eta * mine
    squares = lax.psum(jnp.sum(update * update, axis=1), "gz")
    eigen_new = update / jnp.sqrt(squares[:, None] / geo.pixels + 1e-06)
    return coefficients, eigen_new


def fused_kernel(
    geo, half, flux_hbm, off_ref, word_hbm, eigen_hbm, plan_ref, coef_ref, new_ref,
    pf, pm, phl, est, flux_ref, word_ref, table, grad, incoming,
    row_out, row_in, coef_out, coef_in, local_done,
    table_sent, table_got, grad_sent, grad_got, row_sent, row_got, coef_sent, coef_got,
):
    me = lax.axis_index("gz")
    devices, rank, rows = geo.devices, geo.rank, geo.rows
    shard = geo.pixels // devices
    per = shard // LANES
    low, high, first, last = geo.ranges(me)

    def peers(body):
        def step(k, carry):
            body(lax.rem(me + k, devices))
            return carry

        lax.fori_loop(1, devices, step, 0)

    def others(start, stop, body):
        def step(k, carry):
            @pl.when(k != me)
            def _():
                body(k)

            return carry

        lax.fori_loop(start, stop, step, 0)

    def table_copy(peer, owner):
        return pltpu.make_async_remote_copy(
            src_ref=eigen_hbm,
            dst_ref=table.at[:, columns(owner * per, per)],
            send_sem=table_sent.at[peer],
            recv_sem=table_got.at[owner],
            device_id={"gz": peer},
            device_id_type=pl.DeviceIdType.MESH,
        )

    def grad_copy(owner, source):
        return pltpu.make_async_remote_copy(
            src_ref=grad.at[:, columns(owner * per, per)],
            dst_ref=incoming.at[source],
            send_sem=grad_sent.at[owner],
            recv_sem=grad_got.at[source],
            device_id={"gz": owner},
            device_id_type=pl.DeviceIdType.MESH,
        )

    def row_copy(peer, source):
        return pltpu.make_async_remote_copy(
            src_ref=row_out,
            dst_ref=row_in.at[source],
            send_sem=row_sent.at[peer],
            recv_sem=row_got.at[source],
            device_id={"gz": peer},
            device_id_type=pl.DeviceIdType.MESH,
        )

    copies = [
        pltpu.make_async_copy(flux_hbm, flux_ref, local_done.at[0]),
        pltpu.make_async_copy(word_hbm, word_ref, local_done.at[1]),
        pltpu.make_async_copy(eigen_hbm, table.at[:, columns(me * per, per)], local_done.at[2]),
    ]
    for copy in copies:
        copy.start()
    barrier = pltpu.get_barrier_semaphore()
    peers(lambda peer: pl.semaphore_signal(
        barrier, inc=1, device_id={"gz": peer}, device_id_type=pl.DeviceIdType.MESH
    ))
    pl.semaphore_wait(barrier, devices - 1)
    def send(i, carry):
        half_way = lax.div(i, 2)
        peer = jnp.where(lax.rem(i, 2) == 0, first + half_way, last - half_way)

        @pl.when(peer != me)
        def _():
            table_copy(peer, me).start()

        return carry

    lax.fori_loop(0, last - first + 1, send, 0)
    grad[...] = jnp.zeros_like(grad)
    copies[0].wait()
    copies[1].wait()
    place(geo, me, flux_ref, off_ref, word_ref, pf, pm, phl)
    copies[2].wait()

    def receive(i, carry):
        turn = me + i
        owner = jnp.where(turn > high, turn - (high + 1 - low), turn)

        @pl.when(owner != me)
        def _():
            table_copy(owner, owner).wait_recv()

        split_table(rank, table, est, columns(owner * per, per))
        return carry

    lax.fori_loop(0, high + 1 - low, receive, 0)
    begun = [low]

    def after(chunk, done):
        stop = high + 1 if done else lax.div(chunk, per)
        others(begun[0], stop, lambda owner: grad_copy(owner, me).start())
        begun[0] = stop

    coef = solve(geo, me, pf, pm, phl, est, grad, after)

    padded = jnp.concatenate([coef, jnp.zeros((rows, LANES - rank), jnp.float32)], axis=1)
    lane = lax.broadcasted_iota(jnp.int32, (BS, LANES), 1)
    row = lax.broadcasted_iota(jnp.int32, (BS, LANES), 0)
    plan_row = lax.rem(me, half)
    source, block = plan_ref[0, plan_row], plan_ref[2, plan_row]
    group = LANES // rank
    for h in range(BS // group):
        here = row == lax.div(lane, rank) + h * group
        cols = pl.ds(h * LANES, LANES)
        sent = jnp.zeros((1, LANES), jnp.float32)
        for b in range(NB):
            spread = lane_take(padded[b * BS:(b + 1) * BS], lane & (rank - 1))
            flat = jnp.sum(jnp.where(here, spread, 0.0), axis=0, keepdims=True)
            planned = jnp.where(block == b, 1.0, 0.0)
            gone = planned * jnp.where(source == me, 1.0, 0.0)
            sent = sent + flat * planned
            coef_ref[0, pl.ds(b, 1), cols] = flat * (1.0 - gone)
        coef_out[:, cols] = sent
    partner = lax.rem(me + half, devices)
    coef_copy = pltpu.make_async_remote_copy(
        src_ref=coef_out,
        dst_ref=coef_in,
        send_sem=coef_sent,
        recv_sem=coef_got,
        device_id={"gz": partner},
        device_id_type=pl.DeviceIdType.MESH,
    )
    coef_copy.start()

    new_ref[...] = grad[:, columns(me * per, per)]

    def add(peer):
        grad_copy(me, peer).wait_recv()
        new_ref[...] += incoming[peer]

    others(first, last + 1, add)
    update = table[:, columns(me * per, per)] + geo.eta * new_ref[...]
    new_ref[...] = update
    squares = jnp.sum(update * update, axis=1, keepdims=True)
    wide = lax.broadcasted_iota(jnp.int32, (rank, LANES), 1)
    tall = lax.broadcasted_iota(jnp.int32, (rank, LANES), 0)
    diagonal = wide == tall
    packed = jnp.sum(jnp.where(diagonal, squares, 0.0), axis=0, keepdims=True)
    row_out[...] = packed
    peers(lambda peer: row_copy(peer, me).start())
    coef_copy.wait()
    coef_ref[0, pl.ds(NB, 1), :] = coef_in[...] * jnp.where(source == me, 0.0, 1.0)
    row_in[me] = packed
    peers(lambda peer: row_copy(peer, peer).wait_recv())
    total = row_in[0]
    for d in range(1, devices):
        total = total + row_in[d]
    mean = jnp.sum(jnp.where(diagonal, total, 0.0), axis=1, keepdims=True) / geo.pixels
    new_ref[...] = new_ref[...] / jnp.sqrt(mean + 1e-06)

    peers(lambda peer: row_copy(peer, me).wait_send())
    others(first, last + 1, lambda peer: table_copy(peer, me).wait_send())
    others(low, high + 1, lambda owner: grad_copy(owner, me).wait_send())


def fused(geo, spectra, offsets, mask_bits, eigen, plan):
    vmem = pl.BlockSpec(memory_space=pltpu.VMEM)
    smem = pl.BlockSpec(memory_space=pltpu.SMEM)
    hbm = pl.BlockSpec(memory_space=pltpu.HBM)
    shard = geo.pixels // geo.devices
    width = BS * geo.rank
    many = pltpu.SemaphoreType.DMA((geo.devices,))
    one = pltpu.SemaphoreType.DMA
    return pl.pallas_call(
        functools.partial(fused_kernel, geo, plan.shape[0]),
        out_shape=(
            jax.ShapeDtypeStruct((1, NB + 1, width), jnp.float32),
            jax.ShapeDtypeStruct((geo.rank, shard), jnp.float32),
        ),
        in_specs=[hbm, smem, hbm, hbm, smem],
        out_specs=(vmem, vmem),
        scratch_shapes=window_scratch(geo) + [
            pltpu.VMEM(spectra.shape, jnp.float32),
            pltpu.VMEM(mask_bits.shape, jnp.int32),
            pltpu.VMEM((geo.rank, geo.pixels), jnp.float32),
            pltpu.VMEM((geo.rank, geo.pixels), jnp.float32),
            pltpu.VMEM((geo.devices, geo.rank, shard), jnp.float32),
            pltpu.VMEM((1, LANES), jnp.float32),
            pltpu.VMEM((geo.devices, 1, LANES), jnp.float32),
            pltpu.VMEM((1, width), jnp.float32),
            pltpu.VMEM((1, width), jnp.float32),
            pltpu.SemaphoreType.DMA((3,)),
            many, many, many, many, many, many, one, one,
        ],
        compiler_params=pltpu.CompilerParams(
            vmem_limit_bytes=53 << 20, collective_id=0, has_side_effects=True
        ),
    )(spectra, offsets, mask_bits, eigen, plan.T)


def local(spectra, offsets, mask_bits, eigen, plan):
    devices = lax.axis_size("gz")
    rank, shard = eigen.shape
    geo = Geometry(devices, spectra.shape[0], spectra.shape[1], shard * devices, rank)
    if shard % LANES == 0:
        return fused(geo, spectra, offsets, mask_bits, eigen, plan)
    return plain(geo, spectra, offsets, mask_bits, eigen, plan)


def solution(mesh):
    placed = (
        P(("grp", "gz"), None),
        P(("grp", "gz")),
        P(("grp", "gz"), None),
        P(None, "gz"),
        P("grp", None),
    )
    return jax.shard_map(
        local,
        mesh=mesh,
        in_specs=placed,
        out_specs=(P(("grp", "gz"), None, None), P("grp", "gz")),
        check_vma=False,
    )
```
